256 devices in a mesh: tower: 2 (over core), depth: 32 (over y, z), sub: 4 (over x).
Axes of the slice: x: 4, y: 4, z: 8, core: 2. Of those that a mesh axis runs over, the one named last changes fastest.
Arguments:
- embeds: bfloat16 [2, 131072, 1024], P('tower', ('depth', 'sub')), may hold values from -700 to 700
- counts: int32 [128], P(('depth', 'sub')), may hold values from 256 to 1024, as said below
Outputs:
- row_grads: bfloat16 [2, 131072, 1024], P('tower', ('depth', 'sub'))
- corr_mean: float32 [], replicated
The draws below stay inside these ranges and needn't reach their ends.
Inputs may be any that keep to these rules, and one draw needn't show every extreme that they name: `counts`: block b holds at least 256 and at most 256 + 768 * b // 127 valid samples; the first block holds exactly 256 and the last block is full.
All inputs are finite; a program needn't handle non-finite values.
Results may differ from the reference program's by a relative error of at most 0.022.
Values may be sent and summed in bfloat16 or wider, within the bound.
A program may use at most 128 MiB of HBM per device.

```python
import math
import jax
import jax.numpy as jnp
from jax import lax

O = 1024
ROWS_DEV = 1024
BLOCKS = 128
SAMPLES = 131072


def draw_embeds(key, part):
    keys_list = [jax.random.fold_in(key, 11 + step) for step in range(6)]
    shared = jax.random.truncated_normal(keys_list[0], -4.0, 4.0, (SAMPLES, O), jnp.float32)
    noise_pair = jax.random.truncated_normal(keys_list[1], -4.0, 4.0, (2, SAMPLES, O), jnp.float32)
    row_low = 0.5
    row_high = 2.0
    log_part = 0.8 * shared + 0.6 * noise_pair[0]
    image_part = 0.5 * shared + 0.5 * jnp.roll(shared, 37, axis=1) + 0.7 * noise_pair[1]
    stacked = jnp.stack([log_part, image_part])
    column_scale = jnp.exp(jax.random.uniform(keys_list[3], (2, 1, O), jnp.float32, math.log(0.3), math.log(3.0)))
    row_scale = jnp.exp(jax.random.uniform(keys_list[4], (1, SAMPLES, 1), jnp.float32, math.log(row_low), math.log(row_high)))
    block_index = (jnp.arange(SAMPLES, dtype=jnp.int32) // ROWS_DEV).astype(jnp.float32)
    depth_ramp = jnp.exp(math.log(12.0) * block_index / max(BLOCKS - 1, 1))
    return (stacked * column_scale * row_scale * depth_ramp[None, :, None]).astype(jnp.bfloat16)


def draw_counts(key, part):
    block_index = jnp.arange(BLOCKS, dtype=jnp.int32)
    upper_bound = ROWS_DEV // 4 + 1 + 3 * ROWS_DEV // 4 * block_index // max(BLOCKS - 1, 1)
    drawn_counts = jax.random.randint(jax.random.fold_in(key, 5), (BLOCKS,), ROWS_DEV // 4, upper_bound, dtype=jnp.int32)
    return jnp.where(block_index == BLOCKS - 1, ROWS_DEV, drawn_counts).astype(jnp.int32)


def setup_inputs(seed: int = 0) -> dict:
    key_list = jax.random.split(jax.random.key(seed), 3)
    embeds = draw_embeds(jax.random.fold_in(key_list[2], 71), 0)
    counts = draw_counts(jax.random.fold_in(key_list[2], 71), 0)
    return dict(embeds=embeds, counts=counts)


REG = 0.001
contract_rows = (((0,), (0,)), ((), ()))

def whitening(block_rows, valid_rows, gram_total, column_sum, count_total):
    feature_width = block_rows.shape[1]
    column_mean = column_sum / count_total
    covariance = (gram_total - jnp.outer(column_sum, column_mean)) / (count_total - 1.0) + REG * jnp.eye(feature_width, dtype=jnp.float32)
    factor_lower = jnp.linalg.cholesky(covariance)
    centered = jnp.where(valid_rows[:, None], block_rows.astype(jnp.float32) - column_mean[None, :], 0.0)
    whitened = jax.scipy.linalg.solve_triangular(factor_lower, centered.T, lower=True).T
    return (whitened.astype(jnp.bfloat16), factor_lower)

def tower_stats(block_rows, valid_rows):
    masked = jnp.where(valid_rows[:, None], block_rows, jnp.zeros_like(block_rows))
    gram_total = lax.dot_general(masked.astype(jnp.float32), masked.astype(jnp.float32), contract_rows, preferred_element_type=jnp.float32)
    column_sum = jnp.sum(masked, axis=0, dtype=jnp.float32)
    return (gram_total, column_sum)

def gradient_rows(own_white, other_white, turned, factor_lower, valid_rows):
    product_rows = jnp.dot(own_white.astype(jnp.float32), turned.astype(jnp.float32), preferred_element_type=jnp.float32)
    residual = (other_white.astype(jnp.float32) - product_rows).astype(jnp.bfloat16)
    back_rows = lax.dot_general(residual.astype(jnp.float32), turned.astype(jnp.float32), (((1,), (1,)), ((), ())), preferred_element_type=jnp.float32)
    solved = jax.scipy.linalg.solve_triangular(factor_lower, back_rows.T, lower=True, trans=1).T
    return jnp.where(valid_rows[:, None], solved, 0.0).astype(jnp.bfloat16)

def reference(embeds, counts):
    sample_count = embeds.shape[1]
    feature_width = embeds.shape[2]
    slot_index = jnp.arange(sample_count, dtype=jnp.int32)
    row_limit = jnp.repeat(counts.astype(jnp.int32), ROWS_DEV)
    valid_rows = slot_index % ROWS_DEV < row_limit
    count_total = jnp.sum(counts).astype(jnp.float32)
    log_gram, log_sum = tower_stats(embeds[0], valid_rows)
    image_gram, image_sum = tower_stats(embeds[1], valid_rows)
    log_white, log_lower = whitening(embeds[0], valid_rows, log_gram, log_sum, count_total)
    image_white, image_lower = whitening(embeds[1], valid_rows, image_gram, image_sum, count_total)
    cross = lax.dot_general(log_white.astype(jnp.float32), image_white.astype(jnp.float32), contract_rows, preferred_element_type=jnp.float32) / (count_total - 1.0)
    cross_bf = cross.astype(jnp.bfloat16)
    corr_mean = jnp.sum(jnp.square(cross_bf.astype(jnp.float32))) / feature_width
    log_grad = gradient_rows(log_white, image_white, cross_bf, log_lower, valid_rows)
    image_grad = gradient_rows(image_white, log_white, cross_bf.T, image_lower, valid_rows)
    return (jnp.stack([log_grad, image_grad]), corr_mean)
```

```python
import functools

import jax
import jax.numpy as jnp
from jax import lax
from jax.experimental import pallas as pl
from jax.experimental.pallas import tpu as pltpu
from jax.sharding import PartitionSpec as P

REG = 0.001
MESH = pl.DeviceIdType.MESH
F32, BF16 = jnp.float32, jnp.bfloat16
WIDTH = 1024
HALF = WIDTH // 2
TN = (((0,), (0,)), ((), ()))
NN = (((1,), (0,)), ((), ()))
NT = (((1,), (1,)), ((), ()))
SUB, YS, ZS = 4, 4, 8
BLOCK = 128


def moments_kernel(
    count_ref, x_ref, q_out, c_out, e_out, other_out,
    own, own_t, raw, q_src, c_src, first_in, first_sum, second_in, second_sum, third_in,
    e_x, e_y, e_z, sends, recvs, e_sends, e_recvs, pair_sends, pair_recvs,
):
    tower = lax.axis_index("tower")
    depth = lax.axis_index("depth")
    x = lax.axis_index("sub")
    y, z = depth // ZS, lax.rem(depth, ZS)
    rows = x_ref.shape[0]

    def at_x(p):
        return (tower, depth, p)

    def at_y(p):
        return (tower, p * ZS + z, x)

    def at_z(p):
        return (tower, y * ZS + p, x)

    partner = (1 - tower, depth, x)
    barrier = pltpu.get_barrier_semaphore()
    peers = [partner]
    peers += [at_x(lax.rem(x + d, SUB)) for d in range(1, SUB)]
    peers += [at_y(lax.rem(y + d, YS)) for d in range(1, YS)]
    peers += [at_z(lax.rem(z + d, ZS)) for d in range(1, ZS)]
    for peer in peers:
        pl.semaphore_signal(barrier, inc=1, device_id=peer, device_id_type=MESH)
    pl.semaphore_wait(barrier, len(peers))

    def remote(src, dst, send, recv, device):
        return pltpu.make_async_remote_copy(
            src_ref=src, dst_ref=dst, send_sem=send, recv_sem=recv, device_id=device, device_id_type=MESH
        )

    swap = remote(x_ref, raw, pair_sends.at[0], pair_recvs.at[0], partner)
    swap.start()

    count = count_ref[0]

    def mask_into(src, dst):
        def body(i, carry):
            part = pl.ds(pl.multiple_of(i * 128, 128), 128)
            row = lax.broadcasted_iota(jnp.int32, (128, WIDTH), 0) + i * 128
            dst[part, :] = jnp.where(row < count, src[part, :].astype(F32), 0.0).astype(BF16)
            return carry

        lax.fori_loop(0, rows // 128, body, 0)

    def dot(a, b):
        return jnp.dot(a, b, preferred_element_type=F32)

    mask_into(x_ref, own)

    def turn(i, carry):
        part = pl.ds(pl.multiple_of(i * 128, 128), 128)
        own_t[part, :] = own[:, part].T
        return carry

    lax.fori_loop(0, WIDTH // 128, turn, 0)
    upper = dot(own_t[:HALF, :], own[:, :HALF])
    lower = dot(own_t[HALF:, :], own[:, HALF:])
    r = lax.broadcasted_iota(jnp.int32, (HALF, HALF), 0)
    c = lax.broadcasted_iota(jnp.int32, (HALF, HALF), 1)
    q_src[:, :HALF] = jnp.where(r >= c, upper, lower)
    diagonal = jnp.sum(jnp.where(r == c, lower, 0.0), axis=0, keepdims=True)
    q_src[:, HALF:] = dot(own_t[HALF:, :], own[:, :HALF])

    streams = [(q_src, q_out, 0), (q_src, q_out, 1)]
    cross_out = c_out.at[tower]
    streams += [(c_src, cross_out, 0), (c_src, cross_out, 1)]

    def place(half):
        return ((x, at_x), (y, at_y)) if half == 0 else ((y, at_y), (x, at_x))

    def first(s):
        src, _, half = streams[s]
        (me, at), _ = place(half)
        copies = []
        for d in range(1, 4):
            to = lax.rem(me + d, 4)
            part = pl.ds(pl.multiple_of(half * 256 + to * 64, 64), 64)
            copies.append(remote(src.at[part, :], first_in.at[s, d - 1], sends.at[s, d - 1], recvs.at[s, d - 1], at(to)))
        return copies

    def second(s):
        _, _, half = streams[s]
        _, (me, at) = place(half)
        copies = []
        for d in range(1, 4):
            to = lax.rem(me + d, 4)
            part = pl.ds(pl.multiple_of(to * 16, 16), 16)
            copies.append(remote(first_sum.at[s, part, :], second_in.at[s, d - 1], sends.at[s, d + 2], recvs.at[s, d + 2], at(to)))
        return copies

    def third(s):
        copies = []
        for d in range(1, ZS):
            to = lax.rem(z + d, ZS)
            part = pl.ds(pl.multiple_of(to * 128, 128), 128)
            copies.append(remote(second_sum.at[s, :, part], third_in.at[s, d - 1], sends.at[s, d + 5], recvs.at[s, d + 5], at_z(to)))
        return copies

    def spot(s):
        _, out, half = streams[s]
        (p, _), (q, _) = place(half)
        return out, half * 256 + p * 64, half * 256 + p * 64 + q * 16

    def gather_third(s):
        out, _, row = spot(s)
        here = out.at[pl.ds(pl.multiple_of(row, 16), 16), pl.ds(pl.multiple_of(z * 128, 128), 128)]
        return [remote(here, here, sends.at[s, d + 12], recvs.at[s, d + 12], at_z(lax.rem(z + d, ZS))) for d in range(1, ZS)]

    def gather_second(s):
        out, _, row = spot(s)
        _, (me, at) = place(streams[s][2])
        here = out.at[pl.ds(pl.multiple_of(row, 16), 16), :]
        return [remote(here, here, sends.at[s, d + 19], recvs.at[s, d + 19], at(lax.rem(me + d, 4))) for d in range(1, 4)]

    def gather_first(s):
        out, row, _ = spot(s)
        (me, at), _ = place(streams[s][2])
        here = out.at[pl.ds(pl.multiple_of(row, 64), 64), :]
        return [remote(here, here, sends.at[s, d + 22], recvs.at[s, d + 22], at(lax.rem(me + d, 4))) for d in range(1, 4)]

    def start(copies):
        for copy in copies:
            copy.start()
        return copies

    def arrive(copies):
        for copy in copies:
            copy.wait()

    def sum_first(s):
        src, _, half = streams[s]
        (me, _), _ = place(half)
        part = pl.ds(pl.multiple_of(half * 256 + me * 64, 64), 64)
        first_sum[s] = (src[part, :] + first_in[s, 0]) + (first_in[s, 1] + first_in[s, 2])

    def sum_second(s):
        _, (me, _) = place(streams[s][2])
        part = pl.ds(pl.multiple_of(me * 16, 16), 16)
        second_sum[s] = (first_sum[s, part, :] + second_in[s, 0]) + (second_in[s, 1] + second_in[s, 2])

    def sum_third(s):
        out, _, row = spot(s)
        part = pl.ds(pl.multiple_of(z * 128, 128), 128)
        total = second_sum[s, :, part]
        for d in range(ZS - 1):
            total = total + third_in[s, d]
        out[pl.ds(pl.multiple_of(row, 16), 16), part] = total

    q_first = [start(first(s)) for s in (0, 1)]

    swap.wait()
    mask_into(raw, other_out)
    ones = jnp.ones((8, rows), BF16)
    own_sum = dot(ones, own[...])[:1]
    other_sum = dot(ones, other_out[...])[:1]
    is_log = tower == 0
    e_x[x] = jnp.concatenate(
        [
            jnp.where(is_log, own_sum, other_sum),
            jnp.where(is_log, other_sum, own_sum),
            jnp.concatenate([diagonal, diagonal], axis=1),
            jnp.full((5, WIDTH), count, jnp.int32).astype(F32),
        ],
        axis=0,
    )
    e_copies = start(
        [remote(e_x.at[x], e_x.at[x], e_sends.at[d - 1], e_recvs.at[d - 1], at_x(lax.rem(x + d, SUB))) for d in range(1, SUB)]
    )

    @pl.when(is_log)
    def _():
        c_src[...] = dot(own_t[:HALF, :], other_out[...])

    @pl.when(tower == 1)
    def _():
        c_src[...] = lax.dot_general(other_out[:, HALF:], own[...], TN, preferred_element_type=F32)

    c_first = [start(first(s)) for s in (2, 3)]

    arrive(e_copies)
    e_y[y] = (e_x[0] + e_x[1]) + (e_x[2] + e_x[3])
    e_copies = start(
        [remote(e_y.at[y], e_y.at[y], e_sends.at[d + 2], e_recvs.at[d + 2], at_y(lax.rem(y + d, YS))) for d in range(1, YS)]
    )
    moving = {}
    for s, copies in zip((0, 1), q_first):
        arrive(copies)
        sum_first(s)
        moving[s] = start(second(s))
    arrive(e_copies)
    e_z[z] = (e_y[0] + e_y[1]) + (e_y[2] + e_y[3])
    e_copies = start(
        [remote(e_z.at[z], e_z.at[z], e_sends.at[d + 5], e_recvs.at[d + 5], at_z(lax.rem(z + d, ZS))) for d in range(1, ZS)]
    )
    for s in (0, 1):
        arrive(moving[s])
        sum_second(s)
        moving[s] = start(third(s))
    for s in (0, 1):
        arrive(moving[s])
        sum_third(s)
        moving[s] = start(gather_third(s))
    for s, copies in zip((2, 3), c_first):
        arrive(copies)
        sum_first(s)
        moving[s] = start(second(s))
    for s in (0, 1):
        arrive(moving[s])
        moving[s] = start(gather_second(s))
    for s in (2, 3):
        arrive(moving[s])
        sum_second(s)
        moving[s] = start(third(s))
    for s in (0, 1):
        arrive(moving[s])
        moving[s] = start(gather_first(s))
    for s in (2, 3):
        arrive(moving[s])
        sum_third(s)
        moving[s] = start(gather_third(s))
    for s in (2, 3):
        arrive(moving[s])
        moving[s] = start(gather_second(s))
    for s in (2, 3):
        arrive(moving[s])
        moving[s] = start(gather_first(s))
    arrive(e_copies)
    total = e_z[0]
    for d in range(1, ZS):
        total = total + e_z[d]
    e_out[...] = total
    for s in (0, 1):
        arrive(moving[s])
    for s in (2, 3):
        arrive(moving[s])
    across = remote(cross_out, cross_out, pair_sends.at[1], pair_recvs.at[1], partner)
    across.start()
    across.wait()


def moments(block_rows, counts):
    vmem = pl.BlockSpec(memory_space=pltpu.VMEM)
    rows = block_rows.shape[0]
    dma = pltpu.SemaphoreType.DMA
    return pl.pallas_call(
        moments_kernel,
        out_shape=(
            jax.ShapeDtypeStruct((HALF, WIDTH), F32),
            jax.ShapeDtypeStruct((2, HALF, WIDTH), F32),
            jax.ShapeDtypeStruct((8, WIDTH), F32),
            jax.ShapeDtypeStruct((rows, WIDTH), BF16),
        ),
        in_specs=[pl.BlockSpec(memory_space=pltpu.SMEM), vmem],
        out_specs=(vmem,) * 4,
        scratch_shapes=[
            pltpu.VMEM((rows, WIDTH), BF16),
            pltpu.VMEM((WIDTH, rows), BF16),
            pltpu.VMEM((rows, WIDTH), BF16),
            pltpu.VMEM((HALF, WIDTH), F32),
            pltpu.VMEM((HALF, WIDTH), F32),
            pltpu.VMEM((4, 3, 64, WIDTH), F32),
            pltpu.VMEM((4, 64, WIDTH), F32),
            pltpu.VMEM((4, 3, 16, WIDTH), F32),
            pltpu.VMEM((4, 16, WIDTH), F32),
            pltpu.VMEM((4, 7, 16, 128), F32),
            pltpu.VMEM((SUB, 8, WIDTH), F32),
            pltpu.VMEM((YS, 8, WIDTH), F32),
            pltpu.VMEM((ZS, 8, WIDTH), F32),
            dma((4, 26)),
            dma((4, 26)),
            dma((13,)),
            dma((13,)),
            dma((2,)),
            dma((2,)),
        ],
        compiler_params=pltpu.CompilerParams(collective_id=0, has_side_effects=True, vmem_limit_bytes=48 * 2**20),
        name="moments",
    )(counts, block_rows)


def split(value):
    high = value.astype(BF16)
    return high, (value - high.astype(F32)).astype(BF16)


def dot_parts(left, right, dims):
    (lh, ll), (rh, rl) = left, right
    dot = functools.partial(lax.dot_general, dimension_numbers=dims, preferred_element_type=F32)
    return dot(lh, rh) + (dot(lh, rl) + dot(ll, rh))


def dot_wide(left, right, dims=NN):
    return dot_parts(split(left), split(right), dims)


def inverse_block(block):
    width = block.shape[1]
    rows = lax.broadcasted_iota(jnp.int32, (8, width), 0)
    lanes = lax.broadcasted_iota(jnp.int32, (8, width), 1)

    def spread(value):
        return jnp.broadcast_to(value, (8, width))

    def key(i, j):
        return (i, j) if i <= j else (j, i)

    groups = [block[8 * i : 8 * i + 8] for i in range(width // 8)]
    for g, panel in enumerate(groups):
        panel = groups[g]
        first = 8 * g
        columns = [spread(panel[:, first + j : first + j + 1]) for j in range(8)]
        pivot = {(i, j): spread(columns[j][i : i + 1, :]) for j in range(8) for i in range(j + 1)}
        for k in range(8):
            inverse = 1.0 / pivot[k, k]
            old = {i: pivot[key(i, k)] for i in range(8) if i != k}
            scaled = {i: old[i] * inverse for i in old}
            for j in range(8):
                for i in range(j + 1):
                    if i != k and j != k:
                        pivot[i, j] = pivot[i, j] - scaled[i] * old[j]
            for i in old:
                pivot[key(i, k)] = scaled[i]
            pivot[k, k] = -inverse
        turned = []
        for j in range(8):
            column = pivot[key(7, j)]
            for i in range(6, -1, -1):
                column = jnp.where(rows == i, pivot[key(i, j)], column)
            turned.append(-column)
        solved = turned[0] * spread(panel[:1, :])
        for j in range(1, 8):
            solved = solved + turned[j] * spread(panel[j : j + 1, :])
        for j in range(8):
            solved = jnp.where(lanes == first + j, turned[j], solved)
        lines = [spread(solved[j : j + 1, :]) for j in range(8)]
        inside = (lanes >= first) & (lanes < first + 8)
        for i in [*range(g + 1, width // 8), *range(g)]:
            terms = [groups[i][:, first + j : first + j + 1] * lines[j] for j in range(8)]
            even = (terms[0] + terms[2]) + (terms[4] + terms[6])
            odd = (terms[1] + terms[3]) + (terms[5] + terms[7])
            groups[i] = jnp.where(inside, 0.0, groups[i]) - (even + odd)
        groups[g] = solved
    return jnp.concatenate(groups, axis=0)


def as_column(row):
    return jnp.broadcast_to(row, (8, row.shape[1])).T[:, :1]


def inverse_kernel(q_ref, e_ref, a_ref):
    tower = lax.axis_index("tower")
    total = e_ref[3:4, :1]
    sums = e_ref[pl.ds(tower, 1), :]
    column = as_column(sums)
    mean = sums / total
    r = lax.broadcasted_iota(jnp.int32, (HALF, HALF), 0)
    c = lax.broadcasted_iota(jnp.int32, (HALF, HALF), 1)
    eye = jnp.where(r == c, REG, 0.0)

    def covariance(gram, i, j):
        outer = column[i * HALF : (i + 1) * HALF] * mean[:, j * HALF : (j + 1) * HALF]
        value = (gram - outer) / (total - 1.0)
        a_ref[i * HALF : (i + 1) * HALF, j * HALF : (j + 1) * HALF] = value + eye if i == j else value

    shared = q_ref[:, :HALF]
    turned = shared.T
    covariance(jnp.where(r >= c, shared, turned), 0, 0)
    covariance(jnp.where(r == c, e_ref[2:3, :HALF], jnp.where(r > c, turned, shared)), 1, 1)
    covariance(q_ref[:, HALF:], 1, 0)
    covariance(q_ref[:, HALF:].T, 0, 1)

    def step(k, carry):
        here = pl.ds(pl.multiple_of(k * BLOCK, BLOCK), BLOCK)
        inverse = inverse_block(a_ref[here, here])
        side = a_ref[:, here]
        solved = dot_wide(inverse, a_ref[here, :])
        for part in range(4):
            columns = slice(part * 256, (part + 1) * 256)
            a_ref[:, columns] = a_ref[:, columns] - dot_wide(side, solved[:, columns])
        a_ref[:, here] = -dot_wide(side, inverse)
        a_ref[here, :] = solved
        a_ref[here, here] = inverse
        return carry

    lax.fori_loop(0, WIDTH // BLOCK, step, 0)


def cross_covariance(c_ref, e_ref, column, rows, columns):
    total = e_ref[3:4, :1]
    mean = e_ref[1:2, :] / total
    return (c_ref[rows, columns] - column[rows] * mean[:, columns]) / (total - 1.0)


CHUNKS = [slice(i * 256, (i + 1) * 256) for i in range(WIDTH // 256)]
ALL = slice(None)


def residual_kernel(count_ref, a_ref, c_ref, e_ref, own_ref, other_ref, p_high, p_low, r_ref, a_high, a_low):
    tower = lax.axis_index("tower")
    total = e_ref[3:4, :1]
    own_mean = e_ref[pl.ds(tower, 1), :] / total
    other_mean = e_ref[pl.ds(1 - tower, 1), :] / total
    column = as_column(e_ref[0:1, :])
    high, low = split(a_ref[...])
    a_high[...] = high
    a_low[...] = low

    for part in CHUNKS:

        @pl.when(tower == 0)
        def _():
            cross = split(cross_covariance(c_ref, e_ref, column, ALL, part))
            ph, plow = split(dot_parts((a_high[...], a_low[...]), cross, NN))
            p_high[:, part] = ph
            p_low[:, part] = plow

        @pl.when(tower == 1)
        def _():
            cross = split(cross_covariance(c_ref, e_ref, column, part, ALL))
            ph, plow = split(dot_parts((a_high[...], a_low[...]), cross, NT))
            p_high[:, part] = ph
            p_low[:, part] = plow

    rows = own_ref.shape[0]
    valid = lax.broadcasted_iota(jnp.int32, (rows, 256), 0) < count_ref[0]
    for part in CHUNKS:
        ph, plow = p_high[:, part], p_low[:, part]
        shift = dot_parts(split(jnp.broadcast_to(own_mean, (8, WIDTH))), (ph, plow), NN)[:1]
        fitted = jnp.dot(own_ref[...], ph, preferred_element_type=F32) + jnp.dot(
            own_ref[...], plow, preferred_element_type=F32
        )
        left = (other_ref[:, part].astype(F32) - fitted) - (other_mean[:, part] - shift)
        r_ref[:, part] = jnp.where(valid, left, 0.0).astype(BF16)


def back_kernel(a_ref, p_high, p_low, c_ref, e_ref, m_high, m_low, corr_ref, a_high, a_low):
    column = as_column(e_ref[0:1, :])
    high, low = split(a_ref[...])
    a_high[...] = high
    a_low[...] = low
    corr = jnp.zeros((1, 256), F32)
    for part in CHUNKS:
        back = dot_parts((a_high[...], a_low[...]), (p_high[part, :], p_low[part, :]), NT)
        mh, ml = split(back)
        m_high[:, part] = mh
        m_low[:, part] = ml
        cross = cross_covariance(c_ref, e_ref, column, ALL, part)
        corr = corr + jnp.sum(back * cross, axis=0, keepdims=True)
    corr_ref[...] = jnp.broadcast_to(jnp.sum(corr, axis=1, keepdims=True) / WIDTH, (8, 128))


def gradient_kernel(r_ref, m_high, m_low, out_ref):
    for part in CHUNKS:
        value = jnp.dot(r_ref[...], m_high[:, part], preferred_element_type=F32) + jnp.dot(
            r_ref[...], m_low[:, part], preferred_element_type=F32
        )
        out_ref[:, part] = value.astype(BF16)


VMEM = pl.BlockSpec(memory_space=pltpu.VMEM)
SMEM = pl.BlockSpec(memory_space=pltpu.SMEM)


def local_call(kernel, name, shapes, args, passes, scratch=()):
    specs = [SMEM if arg.dtype == jnp.int32 else VMEM for arg in args]
    return pl.pallas_call(
        kernel,
        out_shape=[jax.ShapeDtypeStruct(shape, dtype) for shape, dtype in shapes],
        in_specs=specs,
        out_specs=[VMEM] * len(shapes),
        scratch_shapes=scratch,
        compiler_params=pltpu.CompilerParams(vmem_limit_bytes=56 * 2**20),
        cost_estimate=pl.CostEstimate(
            flops=passes * 2 * WIDTH**3, bytes_accessed=16 * 2**20, transcendentals=0
        ),
        name=name,
    )(*args)


def on_device(embeds, counts):
    square = (WIDTH, WIDTH)
    block_rows = embeds[0]
    gram, cross, sums, other_rows = moments(block_rows, counts)
    cross = cross.reshape(square)
    (inverse,) = local_call(inverse_kernel, "inverse", [(square, F32)], (gram, sums), 30)
    pairs = [(0, 1), (1, 0)]
    other_inverse = lax.ppermute(inverse, "tower", pairs)
    halves = [pltpu.VMEM(square, BF16)] * 2
    p_high, p_low, residual = local_call(
        residual_kernel,
        "residual",
        [(square, BF16), (square, BF16), (block_rows.shape, BF16)],
        (counts, inverse, cross, sums, block_rows, other_rows),
        5,
        halves,
    )
    m_high, m_low, corr = local_call(
        back_kernel,
        "back",
        [(square, BF16), (square, BF16), ((8, 128), F32)],
        (other_inverse, p_high, p_low, cross, sums),
        3,
        halves,
    )
    log_corr = lax.ppermute(corr, "tower", pairs)
    (gradient,) = local_call(gradient_kernel, "gradient", [(block_rows.shape, BF16)], (residual, m_high, m_low), 2)
    corr_mean = jnp.where(lax.axis_index("tower") == 1, corr, log_corr)[0, 0]
    return gradient[None], corr_mean


def solution(mesh):
    placed = (P("tower", ("depth", "sub"), None), P(("depth", "sub")))
    return jax.shard_map(
        on_device,
        mesh=mesh,
        in_specs=placed,
        out_specs=(P("tower", ("depth", "sub"), None), P()),
        check_vma=False,
    )
```

```python
import functools

import jax
import jax.numpy as jnp
from jax import lax
from jax.experimental import pallas as pl
from jax.experimental.pallas import tpu as pltpu
from jax.sharding import PartitionSpec as P

REG = 0.001
MESH = pl.DeviceIdType.MESH
F32, BF16 = jnp.float32, jnp.bfloat16
WIDTH = 1024
HALF = WIDTH // 2
TN = (((0,), (0,)), ((), ()))
NN = (((1,), (0,)), ((), ()))
NT = (((1,), (1,)), ((), ()))
SUB, YS, ZS = 4, 4, 8
BLOCK = 128


def fused_kernel(
    count_ref, x_ref, out_ref, corr_ref,
    own, own_t, raw, other, q_src, q_sum, c_src, c_sum,
    first_in, first_sum, second_in, second_sum, third_in, e_x, e_y, e_z,
    a_ref, a_parts, o_parts, residual, ready, side_parts, line_high, line_low, corr_box,
    sends, recvs, e_sends, e_recvs, pair_sends, pair_recvs,
):
    tower = lax.axis_index("tower")
    depth = lax.axis_index("depth")
    x = lax.axis_index("sub")
    y, z = depth // ZS, lax.rem(depth, ZS)
    rows = x_ref.shape[0]

    def at_x(p):
        return (tower, depth, p)

    def at_y(p):
        return (tower, p * ZS + z, x)

    def at_z(p):
        return (tower, y * ZS + p, x)

    partner = (1 - tower, depth, x)
    barrier = pltpu.get_barrier_semaphore()
    peers = [partner]
    peers += [at_x(lax.rem(x + d, SUB)) for d in range(1, SUB)]
    peers += [at_y(lax.rem(y + d, YS)) for d in range(1, YS)]
    peers += [at_z(lax.rem(z + d, ZS)) for d in range(1, ZS)]
    for peer in peers:
        pl.semaphore_signal(barrier, inc=1, device_id=peer, device_id_type=MESH)
    pl.semaphore_wait(barrier, len(peers))

    def remote(src, dst, send, recv, device):
        return pltpu.make_async_remote_copy(
            src_ref=src, dst_ref=dst, send_sem=send, recv_sem=recv, device_id=device, device_id_type=MESH
        )

    swap = remote(x_ref, raw, pair_sends.at[0], pair_recvs.at[0], partner)
    swap.start()

    count = count_ref[0]

    def mask_into(src, dst):
        def body(i, carry):
            part = pl.ds(pl.multiple_of(i * 128, 128), 128)
            row = lax.broadcasted_iota(jnp.int32, (128, WIDTH), 0) + i * 128
            dst[part, :] = jnp.where(row < count, src[part, :].astype(F32), 0.0).astype(BF16)
            return carry

        lax.fori_loop(0, rows // 128, body, 0)

    def dot(a, b):
        return jnp.dot(a, b, preferred_element_type=F32)

    mask_into(x_ref, own)

    def turn(i, carry):
        part = pl.ds(pl.multiple_of(i * 128, 128), 128)
        own_t[part, :] = own[:, part].T
        return carry

    lax.fori_loop(0, WIDTH // 128, turn, 0)
    upper = dot(own_t[:HALF, :], own[:, :HALF])
    lower = dot(own_t[HALF:, :], own[:, HALF:])
    r = lax.broadcasted_iota(jnp.int32, (HALF, HALF), 0)
    c = lax.broadcasted_iota(jnp.int32, (HALF, HALF), 1)
    q_src[:, :HALF] = jnp.where(r >= c, upper, lower)
    diagonal = jnp.sum(jnp.where(r == c, lower, 0.0), axis=0, keepdims=True)
    q_src[:, HALF:] = dot(own_t[HALF:, :], own[:, :HALF])

    streams = [(q_src, q_sum, 0), (q_src, q_sum, 1)]
    cross_out = c_sum.at[pl.ds(pl.multiple_of(tower * HALF, HALF), HALF), :]
    streams += [(c_src, cross_out, 0), (c_src, cross_out, 1)]

    def place(half):
        return ((x, at_x), (y, at_y)) if half == 0 else ((y, at_y), (x, at_x))

    def first(s):
        src, _, half = streams[s]
        (me, at), _ = place(half)
        copies = []
        for d in range(1, 4):
            to = lax.rem(me + d, 4)
            part = pl.ds(pl.multiple_of(half * 256 + to * 64, 64), 64)
            copies.append(remote(src.at[part, :], first_in.at[s, d - 1], sends.at[s, d - 1], recvs.at[s, d - 1], at(to)))
        return copies

    def second(s):
        _, _, half = streams[s]
        _, (me, at) = place(half)
        copies = []
        for d in range(1, 4):
            to = lax.rem(me + d, 4)
            part = pl.ds(pl.multiple_of(to * 16, 16), 16)
            copies.append(remote(first_sum.at[s, part, :], second_in.at[s, d - 1], sends.at[s, d + 2], recvs.at[s, d + 2], at(to)))
        return copies

    def third(s):
        copies = []
        for d in range(1, ZS):
            to = lax.rem(z + d, ZS)
            part = pl.ds(pl.multiple_of(to * 128, 128), 128)
            copies.append(remote(second_sum.at[s, :, part], third_in.at[s, d - 1], sends.at[s, d + 5], recvs.at[s, d + 5], at_z(to)))
        return copies

    def spot(s):
        _, out, half = streams[s]
        (p, _), (q, _) = place(half)
        return out, half * 256 + p * 64, half * 256 + p * 64 + q * 16

    def gather_third(s):
        out, _, row = spot(s)
        here = out.at[pl.ds(pl.multiple_of(row, 16), 16), pl.ds(pl.multiple_of(z * 128, 128), 128)]
        return [remote(here, here, sends.at[s, d + 12], recvs.at[s, d + 12], at_z(lax.rem(z + d, ZS))) for d in range(1, ZS)]

    def gather_second(s):
        out, _, row = spot(s)
        _, (me, at) = place(streams[s][2])
        here = out.at[pl.ds(pl.multiple_of(row, 16), 16), :]
        return [remote(here, here, sends.at[s, d + 19], recvs.at[s, d + 19], at(lax.rem(me + d, 4))) for d in range(1, 4)]

    def gather_first(s):
        out, row, _ = spot(s)
        (me, at), _ = place(streams[s][2])
        here = out.at[pl.ds(pl.multiple_of(row, 64), 64), :]
        return [remote(here, here, sends.at[s, d + 22], recvs.at[s, d + 22], at(lax.rem(me + d, 4))) for d in range(1, 4)]

    def start(copies):
        for copy in copies:
            copy.start()
        return copies

    def arrive(copies):
        for copy in copies:
            copy.wait()

    def sum_first(s):
        src, _, half = streams[s]
        (me, _), _ = place(half)
        part = pl.ds(pl.multiple_of(half * 256 + me * 64, 64), 64)
        first_sum[s] = (src[part, :] + first_in[s, 0]) + (first_in[s, 1] + first_in[s, 2])

    def sum_second(s):
        _, (me, _) = place(streams[s][2])
        part = pl.ds(pl.multiple_of(me * 16, 16), 16)
        second_sum[s] = (first_sum[s, part, :] + second_in[s, 0]) + (second_in[s, 1] + second_in[s, 2])

    def sum_third(s):
        out, _, row = spot(s)
        part = pl.ds(pl.multiple_of(z * 128, 128), 128)
        total = second_sum[s, :, part]
        for d in range(ZS - 1):
            total = total + third_in[s, d]
        out[pl.ds(pl.multiple_of(row, 16), 16), part] = total

    q_first = [start(first(s)) for s in (0, 1)]

    swap.wait()
    mask_into(raw, other)
    ones = jnp.ones((8, rows), BF16)
    own_sum = dot(ones, own[...])[:1]
    other_sum = dot(ones, other[...])[:1]
    is_log = tower == 0
    e_x[x] = jnp.concatenate(
        [
            jnp.where(is_log, own_sum, other_sum),
            jnp.where(is_log, other_sum, own_sum),
            jnp.concatenate([diagonal, diagonal], axis=1),
            jnp.full((5, WIDTH), count, jnp.int32).astype(F32),
        ],
        axis=0,
    )
    e_copies = start(
        [remote(e_x.at[x], e_x.at[x], e_sends.at[d - 1], e_recvs.at[d - 1], at_x(lax.rem(x + d, SUB))) for d in range(1, SUB)]
    )

    @pl.when(is_log)
    def _():
        c_src[...] = dot(own_t[:HALF, :], other[...])

    @pl.when(tower == 1)
    def _():
        c_src[...] = lax.dot_general(other[:, HALF:], own[...], TN, preferred_element_type=F32)

    arrive(e_copies)
    e_y[y] = (e_x[0] + e_x[1]) + (e_x[2] + e_x[3])
    e_copies = start(
        [remote(e_y.at[y], e_y.at[y], e_sends.at[d + 2], e_recvs.at[d + 2], at_y(lax.rem(y + d, YS))) for d in range(1, YS)]
    )
    moving = {}
    for s, copies in zip((0, 1), q_first):
        arrive(copies)
        sum_first(s)
        moving[s] = start(second(s))
    for s in (2, 3):
        start(first(s))
    arrive(e_copies)
    e_z[z] = (e_y[0] + e_y[1]) + (e_y[2] + e_y[3])
    e_copies = start(
        [remote(e_z.at[z], e_z.at[z], e_sends.at[d + 5], e_recvs.at[d + 5], at_z(lax.rem(z + d, ZS))) for d in range(1, ZS)]
    )
    for s in (0, 1):
        arrive(moving[s])
        sum_second(s)
        moving[s] = start(third(s))
    for s in (0, 1):
        arrive(moving[s])
        sum_third(s)
        moving[s] = start(gather_third(s))
    for s in (0, 1):
        arrive(moving[s])
        moving[s] = start(gather_second(s))
    for s in (0, 1):
        arrive(moving[s])
        moving[s] = start(gather_first(s))
    arrive(e_copies)
    sums = e_z[0]
    for d in range(1, ZS):
        sums = sums + e_z[d]
    for s in (0, 1):
        arrive(moving[s])

    count_total = sums[3:4, :1]
    own_total = jnp.where(is_log, sums[0:1], sums[1:2])
    own_mean = own_total / count_total
    other_mean = jnp.where(is_log, sums[1:2], sums[0:1]) / count_total
    column = as_column(own_total)
    eye = jnp.where(r == c, REG, 0.0)

    def covariance(gram, i, j):
        outer = column[i * HALF : (i + 1) * HALF] * own_mean[:, j * HALF : (j + 1) * HALF]
        value = (gram - outer) / (count_total - 1.0)
        a_ref[i * HALF : (i + 1) * HALF, j * HALF : (j + 1) * HALF] = value + eye if i == j else value

    shared = q_sum[:, :HALF]
    turned = shared.T
    covariance(jnp.where(r >= c, shared, turned), 0, 0)
    covariance(jnp.where(r == c, sums[2:3, :HALF], jnp.where(r > c, turned, shared)), 1, 1)
    covariance(q_sum[:, HALF:], 1, 0)
    covariance(q_sum[:, HALF:].T, 0, 1)

    across = remote(cross_out, cross_out, pair_sends.at[1], pair_recvs.at[1], partner)

    def cross_moves(k):
        @pl.when(k == 0)
        def _():
            for s in (2, 3):
                arrive(first(s))
                sum_first(s)
                start(second(s))

        @pl.when(k == 1)
        def _():
            for s in (2, 3):
                arrive(second(s))
                sum_second(s)
                start(third(s))

        @pl.when(k == 2)
        def _():
            for s in (2, 3):
                arrive(third(s))
                sum_third(s)
                start(gather_third(s))

        @pl.when(k == 3)
        def _():
            for s in (2, 3):
                arrive(gather_third(s))
                start(gather_second(s))

        @pl.when(k == 4)
        def _():
            for s in (2, 3):
                arrive(gather_second(s))
                start(gather_first(s))

        @pl.when(k == 6)
        def _():
            for s in (2, 3):
                arrive(gather_first(s))
            across.start()

    ready[...] = inverse_block(a_ref[:BLOCK, :BLOCK])

    def step(k, carry):
        cross_moves(k)
        here = pl.ds(pl.multiple_of(k * BLOCK, BLOCK), BLOCK)
        after = lax.rem(k + 1, WIDTH // BLOCK) * BLOCK
        after = pl.ds(pl.multiple_of(after, BLOCK), BLOCK)
        inverse = ready[...]
        left = stack_columns(inverse)
        follow = a_ref[after, after] - dot_stacked(
            stack_columns(a_ref[after, here]), stack_rows(dot_stacked(left, stack_rows(a_ref[here, after])))
        )
        side = a_ref[:, here]
        solved = dot_stacked(left, stack_rows(a_ref[here, :]))
        a_ref[:, here] = jnp.zeros((WIDTH, BLOCK), F32)
        a_ref[here, :] = solved
        a_ref[here, here] = inverse
        line_high[...], line_low[...] = stack_rows(a_ref[here, :])
        row = lax.broadcasted_iota(jnp.int32, (WIDTH, BLOCK), 0) - k * BLOCK
        side_parts[...] = stack_columns(jnp.where((row >= 0) & (row < BLOCK), 0.0, side))
        for i in range(4):
            for j in range(4):
                rows_part, columns_part = slice(i * 256, (i + 1) * 256), slice(j * 256, (j + 1) * 256)
                a_ref[rows_part, columns_part] = a_ref[rows_part, columns_part] - dot_stacked(
                    side_parts[rows_part, :], (line_high[:, columns_part], line_low[:, columns_part])
                )
        ready[...] = inverse_block(follow)
        return carry

    lax.fori_loop(0, WIDTH // BLOCK, step, 0)

    for part in CHUNKS:
        high, low = split(a_ref[part, :])
        a_parts[0, part, :] = high
        a_parts[1, part, :] = low
    trade = remote(a_parts, o_parts, pair_sends.at[3], pair_recvs.at[3], partner)
    trade.start()
    across.wait()
    p_high, p_low = own_t, raw
    log_column = as_column(sums[0:1])
    image_mean = sums[1:2] / count_total

    def cross_covariance(some_rows, some_columns):
        outer = log_column[some_rows] * image_mean[:, some_columns]
        return (c_sum[some_rows, some_columns] - outer) / (count_total - 1.0)

    for part in CHUNKS:

        @pl.when(is_log)
        def _():
            cross = split(cross_covariance(ALL, part))
            p_high[:, part], p_low[:, part] = split(dot_parts((a_parts[0], a_parts[1]), cross, NN))

        @pl.when(tower == 1)
        def _():
            cross = split(cross_covariance(part, ALL))
            p_high[:, part], p_low[:, part] = split(dot_parts((a_parts[0], a_parts[1]), cross, NT))

    valid = lax.broadcasted_iota(jnp.int32, (rows, 256), 0) < count
    mean_parts = split(jnp.broadcast_to(own_mean, (8, WIDTH)))
    for part in CHUNKS:
        high, low = p_high[:, part], p_low[:, part]
        shift = dot_parts(mean_parts, (high, low), NN)[:1]
        left = (other[:, part].astype(F32) - (dot(own[...], high) + dot(own[...], low))) - (other_mean[:, part] - shift)
        residual[:, part] = jnp.where(valid, left, 0.0).astype(BF16)

    trade.wait()
    m_high, m_low = a_parts.at[0], a_parts.at[1]
    corr = jnp.zeros((1, 256), F32)
    for part in CHUNKS:
        back = dot_parts((o_parts[0], o_parts[1]), (p_high[part, :], p_low[part, :]), NT)
        m_high[:, part], m_low[:, part] = split(back)
        corr = corr + jnp.sum(back * cross_covariance(ALL, part), axis=0, keepdims=True)
    corr_box[tower] = jnp.broadcast_to(jnp.sum(corr, axis=1, keepdims=True) / WIDTH, (8, 128))
    tell = remote(corr_box.at[tower], corr_box.at[tower], pair_sends.at[2], pair_recvs.at[2], partner)
    tell.start()
    for part in CHUNKS:
        value = dot(residual[...], m_high[:, part]) + dot(residual[...], m_low[:, part])
        out_ref[:, part] = value.astype(BF16)
    tell.wait()
    corr_ref[...] = corr_box[1]


def split(value):
    high = value.astype(BF16)
    return high, (value - high.astype(F32)).astype(BF16)


def dot_parts(left, right, dims):
    (lh, ll), (rh, rl) = left, right
    dot = functools.partial(lax.dot_general, dimension_numbers=dims, preferred_element_type=F32)
    return dot(lh, rh) + (dot(lh, rl) + dot(ll, rh))


def dot_wide(left, right, dims=NN):
    return dot_parts(split(left), split(right), dims)


def inverse_block(block):
    width = block.shape[1]
    rows = lax.broadcasted_iota(jnp.int32, (8, width), 0)
    lanes = lax.broadcasted_iota(jnp.int32, (8, width), 1)

    def spread(value):
        return jnp.broadcast_to(value, (8, width))

    def key(i, j):
        return (i, j) if i <= j else (j, i)

    groups = [block[8 * i : 8 * i + 8] for i in range(width // 8)]
    for g, panel in enumerate(groups):
        panel = groups[g]
        first = 8 * g
        columns = [spread(panel[:, first + j : first + j + 1]) for j in range(8)]
        pivot = {(i, j): spread(columns[j][i : i + 1, :]) for j in range(8) for i in range(j + 1)}
        for k in range(8):
            inverse = 1.0 / pivot[k, k]
            old = {i: pivot[key(i, k)] for i in range(8) if i != k}
            scaled = {i: old[i] * inverse for i in old}
            for j in range(8):
                for i in range(j + 1):
                    if i != k and j != k:
                        pivot[i, j] = pivot[i, j] - scaled[i] * old[j]
            for i in old:
                pivot[key(i, k)] = scaled[i]
            pivot[k, k] = -inverse
        turned = []
        for j in range(8):
            column = pivot[key(7, j)]
            for i in range(6, -1, -1):
                column = jnp.where(rows == i, pivot[key(i, j)], column)
            turned.append(-column)
        solved = turned[0] * spread(panel[:1, :])
        for j in range(1, 8):
            solved = solved + turned[j] * spread(panel[j : j + 1, :])
        for j in range(8):
            solved = jnp.where(lanes == first + j, turned[j], solved)
        lines = [spread(solved[j : j + 1, :]) for j in range(8)]
        inside = (lanes >= first) & (lanes < first + 8)
        for i in [*range(g + 1, width // 8), *range(g)]:
            terms = [groups[i][:, first + j : first + j + 1] * lines[j] for j in range(8)]
            even = (terms[0] + terms[2]) + (terms[4] + terms[6])
            odd = (terms[1] + terms[3]) + (terms[5] + terms[7])
            groups[i] = jnp.where(inside, 0.0, groups[i]) - (even + odd)
        groups[g] = solved
    return jnp.concatenate(groups, axis=0)


def as_column(row):
    return jnp.broadcast_to(row, (8, row.shape[1])).T[:, :1]


def stack_columns(value):
    return jnp.concatenate(split(value), axis=1)


def stack_rows(value):
    high, low = split(value)
    return jnp.concatenate([high, high], axis=0), jnp.concatenate([low, low], axis=0)


def dot_stacked(left, right):
    high, low = right
    dot = functools.partial(jnp.dot, preferred_element_type=F32)
    return dot(left, high) + dot(left, low)


CHUNKS = [slice(i * 256, (i + 1) * 256) for i in range(WIDTH // 256)]
ALL = slice(None)


def on_device(embeds, counts):
    block_rows = embeds[0]
    rows = block_rows.shape[0]
    vmem = pl.BlockSpec(memory_space=pltpu.VMEM)
    dma = pltpu.SemaphoreType.DMA
    half, square = (HALF, WIDTH), (WIDTH, WIDTH)
    gradient, corr = pl.pallas_call(
        fused_kernel,
        out_shape=(jax.ShapeDtypeStruct(block_rows.shape, BF16), jax.ShapeDtypeStruct((8, 128), F32)),
        in_specs=[pl.BlockSpec(memory_space=pltpu.SMEM), vmem],
        out_specs=(vmem, vmem),
        scratch_shapes=[
            pltpu.VMEM((rows, WIDTH), BF16),
            pltpu.VMEM((WIDTH, rows), BF16),
            pltpu.VMEM((rows, WIDTH), BF16),
            pltpu.VMEM((rows, WIDTH), BF16),
            pltpu.VMEM(half, F32),
            pltpu.VMEM(half, F32),
            pltpu.VMEM(half, F32),
            pltpu.VMEM(square, F32),
            pltpu.VMEM((4, 3, 64, WIDTH), F32),
            pltpu.VMEM((4, 64, WIDTH), F32),
            pltpu.VMEM((4, 3, 16, WIDTH), F32),
            pltpu.VMEM((4, 16, WIDTH), F32),
            pltpu.VMEM((4, 7, 16, 128), F32),
            pltpu.VMEM((SUB, 8, WIDTH), F32),
            pltpu.VMEM((YS, 8, WIDTH), F32),
            pltpu.VMEM((ZS, 8, WIDTH), F32),
            pltpu.VMEM(square, F32),
            pltpu.VMEM((2, *square), BF16),
            pltpu.VMEM((2, *square), BF16),
            pltpu.VMEM((rows, WIDTH), BF16),
            pltpu.VMEM((BLOCK, BLOCK), F32),
            pltpu.VMEM((WIDTH, 2 * BLOCK), BF16),
            pltpu.VMEM((2 * BLOCK, WIDTH), BF16),
            pltpu.VMEM((2 * BLOCK, WIDTH), BF16),
            pltpu.VMEM((2, 8, 128), F32),
            dma((4, 26)),
            dma((4, 26)),
            dma((13,)),
            dma((13,)),
            dma((4,)),
            dma((4,)),
        ],
        compiler_params=pltpu.CompilerParams(collective_id=0, has_side_effects=True, vmem_limit_bytes=60 * 2**20),
        name="fused",
    )(counts, block_rows)
    return gradient[None], corr[0, 0]


def solution(mesh):
    placed = (P("tower", ("depth", "sub"), None), P(("depth", "sub")))
    return jax.shard_map(
        on_device,
        mesh=mesh,
        in_specs=placed,
        out_specs=(P("tower", ("depth", "sub"), None), P()),
        check_vma=False,
    )
```

```python
import functools

import jax
import jax.numpy as jnp
from jax import lax
from jax.experimental import pallas as pl
from jax.experimental.pallas import tpu as pltpu
from jax.sharding import PartitionSpec as P

REG = 0.001
MESH = pl.DeviceIdType.MESH
F32, BF16 = jnp.float32, jnp.bfloat16
WIDTH = 1024
HALF = WIDTH // 2
TN = (((0,), (0,)), ((), ()))
NN = (((1,), (0,)), ((), ()))
NT = (((1,), (1,)), ((), ()))
SUB, YS, ZS = 4, 4, 8
BLOCK = 128


def fused_kernel(
    count_ref, x_ref, out_ref, corr_ref,
    own, own_t, raw, other, q_src, q_sum, c_src, c_sum,
    first_in, first_sum, second_in, second_sum, third_in, third_out, e_x, e_y, e_z,
    a_ref, a_parts, o_parts, residual, ready, side_parts, line_high, line_low, corr_box,
    sends, recvs, e_sends, e_recvs, pair_sends, pair_recvs,
):
    tower = lax.axis_index("tower")
    depth = lax.axis_index("depth")
    x = lax.axis_index("sub")
    y, z = depth // ZS, lax.rem(depth, ZS)
    rows = x_ref.shape[0]

    def at_x(p):
        return (tower, depth, p)

    def at_y(p):
        return (tower, p * ZS + z, x)

    def at_z(p):
        return (tower, y * ZS + p, x)

    partner = (1 - tower, depth, x)
    barrier = pltpu.get_barrier_semaphore()
    peers = [partner]
    peers += [at_x(lax.rem(x + d, SUB)) for d in range(1, SUB)]
    peers += [at_y(lax.rem(y + d, YS)) for d in range(1, YS)]
    peers += [at_z(lax.rem(z + d, ZS)) for d in range(1, ZS)]
    for peer in peers:
        pl.semaphore_signal(barrier, inc=1, device_id=peer, device_id_type=MESH)
    def remote(src, dst, send, recv, device):
        return pltpu.make_async_remote_copy(
            src_ref=src, dst_ref=dst, send_sem=send, recv_sem=recv, device_id=device, device_id_type=MESH
        )

    count = count_ref[0]

    def mask_into(src, dst):
        def body(i, carry):
            part = pl.ds(pl.multiple_of(i * 128, 128), 128)
            row = lax.broadcasted_iota(jnp.int32, (128, WIDTH), 0) + i * 128
            dst[part, :] = jnp.where(row < count, src[part, :].astype(F32), 0.0).astype(BF16)
            return carry

        lax.fori_loop(0, rows // 128, body, 0)

    def dot(a, b):
        return jnp.dot(a, b, preferred_element_type=F32)

    mask_into(x_ref, own)

    def turn(i, carry):
        part = pl.ds(pl.multiple_of(i * 128, 128), 128)
        own_t[part, :] = own[:, part].T
        return carry

    lax.fori_loop(0, WIDTH // 128, turn, 0)

    pl.semaphore_wait(barrier, len(peers))
    swap = remote(x_ref, raw, pair_sends.at[0], pair_recvs.at[0], partner)
    swap.start()

    r = lax.broadcasted_iota(jnp.int32, (HALF, HALF), 0)
    c = lax.broadcasted_iota(jnp.int32, (HALF, HALF), 1)

    cross_out = c_sum.at[pl.ds(pl.multiple_of(tower * HALF, HALF), HALF), :]
    streams = [(q_src, q_sum, h, slice(0, HALF)) for h in range(2)]
    streams += [(q_src, q_sum, h, slice(HALF, WIDTH)) for h in range(2)]
    streams += [(c_src, cross_out, h, slice(0, WIDTH)) for h in range(2)]

    def place(s):
        return ((x, at_x), (y, at_y)) if streams[s][2] == 0 else ((y, at_y), (x, at_x))

    def wide(s):
        return slice(0, HALF if s < 4 else WIDTH)

    def rows_of(first_row, size):
        return pl.ds(pl.multiple_of(first_row, size), size)

    def share(s, p):
        if s < 4:
            return rows_of(p // 4 * 8, 8), pl.ds(pl.multiple_of(lax.rem(p, 4) * 128, 128), 128)
        return slice(0, 16), pl.ds(pl.multiple_of(p * 128, 128), 128)

    def link(s, stage, src, dst, device):
        return remote(src, dst, sends.at[s, stage], recvs.at[s, stage], device)

    def first(s):
        src, _, half, columns = streams[s]
        (me, at), _ = place(s)
        copies = []
        for d in range(1, 4):
            to = lax.rem(me + d, 4)
            part = src.at[rows_of(half * 256 + to * 64, 64), columns]
            copies.append(link(s, d - 1, part, first_in.at[s, d - 1, :, wide(s)], at(to)))
        return copies

    def second(s):
        _, (me, at) = place(s)
        copies = []
        for d in range(1, 4):
            to = lax.rem(me + d, 4)
            part = first_sum.at[s, rows_of(to * 16, 16), wide(s)]
            copies.append(link(s, d + 2, part, second_in.at[s, d - 1, :, wide(s)], at(to)))
        return copies

    def third(s):
        copies = []
        for d in range(1, ZS):
            to = lax.rem(z + d, ZS)
            some_rows, columns = share(s, to)
            part = second_sum.at[s : s + 2, some_rows, columns]
            copies.append(link(s, d + 5, part, third_in.at[s // 2, d - 1, :, : 8 if s < 4 else 16, :], at_z(to)))
        return copies

    def spot(s):
        _, out, half, columns = streams[s]
        (p, _), (q, _) = place(s)
        return out, half * 256 + p * 64, half * 256 + p * 64 + q * 16, columns

    def gather_third(s):
        some_rows, columns = share(s, z)
        here = third_out.at[s : s + 2, some_rows, columns]
        return [link(s, d + 12, here, here, at_z(lax.rem(z + d, ZS))) for d in range(1, ZS)]

    def put_third(s):
        out, _, row, columns = spot(s)
        out[rows_of(row, 16), columns] = third_out[s, :, wide(s)]

    def gather_second(s):
        out, _, row, columns = spot(s)
        _, (me, at) = place(s)
        here = out.at[rows_of(row, 16), columns]
        return [link(s, d + 19, here, here, at(lax.rem(me + d, 4))) for d in range(1, 4)]

    def gather_first(s):
        out, row, _, columns = spot(s)
        (me, at), _ = place(s)
        here = out.at[rows_of(row, 64), columns]
        return [link(s, d + 22, here, here, at(lax.rem(me + d, 4))) for d in range(1, 4)]

    def start(copies):
        for copy in copies:
            copy.start()
        return copies

    def arrive(copies):
        for copy in copies:
            copy.wait()

    def sum_first(s):
        src, _, half, columns = streams[s]
        (me, _), _ = place(s)
        mine = src[rows_of(half * 256 + me * 64, 64), columns]
        came = [first_in[s, d, :, wide(s)] for d in range(3)]
        first_sum[s, :, wide(s)] = (mine + came[0]) + (came[1] + came[2])

    def sum_second(s):
        _, (me, _) = place(s)
        mine = first_sum[s, rows_of(me * 16, 16), wide(s)]
        came = [second_in[s, d, :, wide(s)] for d in range(3)]
        second_sum[s, :, wide(s)] = (mine + came[0]) + (came[1] + came[2])

    def sum_third(s):
        some_rows, columns = share(s, z)
        total = second_sum[s : s + 2, some_rows, columns]
        for d in range(ZS - 1):
            total = total + third_in[s // 2, d, :, : 8 if s < 4 else 16, :]
        third_out[s : s + 2, some_rows, columns] = total

    q_first = []
    diagonal = jnp.zeros((1, HALF), F32)
    for h in range(2):
        here, below = slice(h * 256, h * 256 + 256), slice(HALF + h * 256, HALF + h * 256 + 256)
        upper = dot(own_t[here, :], own[:, :HALF])
        lower = dot(own_t[below, :], own[:, HALF:])
        q_src[here, :HALF] = jnp.where(r[here] >= c[here], upper, lower)
        diagonal = diagonal + jnp.sum(jnp.where(r[here] == c[here], lower, 0.0), axis=0, keepdims=True)
        q_first.append(start(first(h)))
    for h in range(2):
        here, below = slice(h * 256, h * 256 + 256), slice(HALF + h * 256, HALF + h * 256 + 256)
        q_src[here, HALF:] = dot(own_t[below, :], own[:, :HALF])
        q_first.append(start(first(2 + h)))

    swap.wait()
    mask_into(raw, other)
    ones = jnp.ones((8, rows), BF16)
    own_sum = dot(ones, own[...])[:1]
    other_sum = dot(ones, other[...])[:1]
    is_log = tower == 0
    e_x[x] = jnp.concatenate(
        [
            jnp.where(is_log, own_sum, other_sum),
            jnp.where(is_log, other_sum, own_sum),
            jnp.concatenate([diagonal, diagonal], axis=1),
            jnp.full((5, WIDTH), count, jnp.int32).astype(F32),
        ],
        axis=0,
    )
    e_copies = start(
        [remote(e_x.at[x], e_x.at[x], e_sends.at[d - 1], e_recvs.at[d - 1], at_x(lax.rem(x + d, SUB))) for d in range(1, SUB)]
    )

    @pl.when(is_log)
    def _():
        c_src[...] = dot(own_t[:HALF, :], other[...])

    @pl.when(tower == 1)
    def _():
        c_src[...] = lax.dot_general(other[:, HALF:], own[...], TN, preferred_element_type=F32)

    arrive(e_copies)
    e_y[y] = (e_x[0] + e_x[1]) + (e_x[2] + e_x[3])
    e_copies = start(
        [remote(e_y.at[y], e_y.at[y], e_sends.at[d + 2], e_recvs.at[d + 2], at_y(lax.rem(y + d, YS))) for d in range(1, YS)]
    )
    for s, copies in enumerate(q_first):
        arrive(copies)
        sum_first(s)
        start(second(s))
    for s in (4, 5):
        start(first(s))
    arrive(e_copies)
    e_z[z] = (e_y[0] + e_y[1]) + (e_y[2] + e_y[3])
    e_copies = start(
        [remote(e_z.at[z], e_z.at[z], e_sends.at[d + 5], e_recvs.at[d + 5], at_z(lax.rem(z + d, ZS))) for d in range(1, ZS)]
    )
    for pair in (0, 2):
        for s in (pair, pair + 1):
            arrive(second(s))
            sum_second(s)
        start(third(pair))
    for pair in (0, 2):
        arrive(third(pair))
        sum_third(pair)
        start(gather_third(pair))
    for pair in (0, 2):
        arrive(gather_third(pair))
        for s in (pair, pair + 1):
            put_third(s)
            start(gather_second(s))
    for s in range(4):
        arrive(gather_second(s))
        start(gather_first(s))
    arrive(e_copies)
    sums = e_z[0]
    for d in range(1, ZS):
        sums = sums + e_z[d]
    for s in (0, 1):
        arrive(gather_first(s))

    count_total = sums[3:4, :1]
    own_total = jnp.where(is_log, sums[0:1], sums[1:2])
    own_mean = own_total / count_total
    other_mean = jnp.where(is_log, sums[1:2], sums[0:1]) / count_total
    column = as_column(own_total)
    eye = jnp.where(r == c, REG, 0.0)

    def covariance(gram, i, j):
        outer = column[i * HALF : (i + 1) * HALF] * own_mean[:, j * HALF : (j + 1) * HALF]
        value = (gram - outer) / (count_total - 1.0)
        a_ref[i * HALF : (i + 1) * HALF, j * HALF : (j + 1) * HALF] = value + eye if i == j else value

    shared = q_sum[:, :HALF]
    turned = shared.T
    covariance(jnp.where(r >= c, shared, turned), 0, 0)
    covariance(jnp.where(r == c, sums[2:3, :HALF], jnp.where(r > c, turned, shared)), 1, 1)
    ready[...] = inverse_block(a_ref[:BLOCK, :BLOCK])
    for s in (2, 3):
        arrive(gather_first(s))
    covariance(q_sum[:, HALF:], 1, 0)
    covariance(q_sum[:, HALF:].T, 0, 1)

    across = remote(cross_out, cross_out, pair_sends.at[1], pair_recvs.at[1], partner)

    def cross_moves(k):
        @pl.when(k == 0)
        def _():
            for s in (4, 5):
                arrive(first(s))
                sum_first(s)
                start(second(s))

        @pl.when(k == 1)
        def _():
            for s in (4, 5):
                arrive(second(s))
                sum_second(s)
            start(third(4))

        @pl.when(k == 2)
        def _():
            arrive(third(4))
            sum_third(4)
            start(gather_third(4))

        @pl.when(k == 3)
        def _():
            arrive(gather_third(4))
            for s in (4, 5):
                put_third(s)
                start(gather_second(s))

        @pl.when(k == 4)
        def _():
            for s in (4, 5):
                arrive(gather_second(s))
                start(gather_first(s))

        @pl.when(k == 6)
        def _():
            for s in (4, 5):
                arrive(gather_first(s))
            across.start()

    def step(k, carry):
        cross_moves(k)
        here = pl.ds(pl.multiple_of(k * BLOCK, BLOCK), BLOCK)
        after = lax.rem(k + 1, WIDTH // BLOCK) * BLOCK
        after = pl.ds(pl.multiple_of(after, BLOCK), BLOCK)
        inverse = ready[...]
        left = stack_columns(inverse)
        follow = a_ref[after, after] - dot_stacked(
            stack_columns(a_ref[after, here]), stack_rows(dot_stacked(left, stack_rows(a_ref[here, after])))
        )
        side = a_ref[:, here]
        solved = dot_stacked(left, stack_rows(a_ref[here, :]))
        a_ref[:, here] = jnp.zeros((WIDTH, BLOCK), F32)
        a_ref[here, :] = solved
        a_ref[here, here] = inverse
        line_high[...], line_low[...] = stack_rows(a_ref[here, :])
        row = lax.broadcasted_iota(jnp.int32, (WIDTH, BLOCK), 0) - k * BLOCK
        side_parts[...] = stack_columns(jnp.where((row >= 0) & (row < BLOCK), 0.0, side))
        for i in range(4):
            for j in range(4):
                rows_part, columns_part = slice(i * 256, (i + 1) * 256), slice(j * 256, (j + 1) * 256)
                a_ref[rows_part, columns_part] = a_ref[rows_part, columns_part] - dot_stacked(
                    side_parts[rows_part, :], (line_high[:, columns_part], line_low[:, columns_part])
                )
        ready[...] = inverse_block(follow)
        return carry

    lax.fori_loop(0, WIDTH // BLOCK, step, 0)

    for part in CHUNKS:
        high, low = split(a_ref[part, :])
        a_parts[0, part, :] = high
        a_parts[1, part, :] = low
    trade = remote(a_parts, o_parts, pair_sends.at[3], pair_recvs.at[3], partner)
    trade.start()
    across.wait()
    p_high, p_low = own_t, raw
    log_column = as_column(sums[0:1])
    image_mean = sums[1:2] / count_total

    def cross_covariance(some_rows, some_columns):
        outer = log_column[some_rows] * image_mean[:, some_columns]
        return (c_sum[some_rows, some_columns] - outer) / (count_total - 1.0)

    for part in CHUNKS:

        @pl.when(is_log)
        def _():
            cross = split(cross_covariance(ALL, part))
            p_high[:, part], p_low[:, part] = split(dot_parts((a_parts[0], a_parts[1]), cross, NN))

        @pl.when(tower == 1)
        def _():
            cross = split(cross_covariance(part, ALL))
            p_high[:, part], p_low[:, part] = split(dot_parts((a_parts[0], a_parts[1]), cross, NT))

    valid = lax.broadcasted_iota(jnp.int32, (rows, 256), 0) < count
    mean_parts = split(jnp.broadcast_to(own_mean, (8, WIDTH)))
    for part in CHUNKS:
        high, low = p_high[:, part], p_low[:, part]
        shift = dot_parts(mean_parts, (high, low), NN)[:1]
        left = (other[:, part].astype(F32) - (dot(own[...], high) + dot(own[...], low))) - (other_mean[:, part] - shift)
        residual[:, part] = jnp.where(valid, left, 0.0).astype(BF16)

    trade.wait()
    m_high, m_low = a_parts.at[0], a_parts.at[1]
    corr = jnp.zeros((1, 256), F32)
    for part in CHUNKS:
        back = dot_parts((o_parts[0], o_parts[1]), (p_high[part, :], p_low[part, :]), NT)
        m_high[:, part], m_low[:, part] = split(back)
        corr = corr + jnp.sum(back * cross_covariance(ALL, part), axis=0, keepdims=True)
    corr_box[tower] = jnp.broadcast_to(jnp.sum(corr, axis=1, keepdims=True) / WIDTH, (8, 128))
    tell = remote(corr_box.at[tower], corr_box.at[tower], pair_sends.at[2], pair_recvs.at[2], partner)
    tell.start()
    for part in CHUNKS:
        value = dot(residual[...], m_high[:, part]) + dot(residual[...], m_low[:, part])
        out_ref[:, part] = value.astype(BF16)
    tell.wait()
    corr_ref[...] = corr_box[1]


def split(value):
    high = value.astype(BF16)
    return high, (value - high.astype(F32)).astype(BF16)


def dot_parts(left, right, dims):
    (lh, ll), (rh, rl) = left, right
    dot = functools.partial(lax.dot_general, dimension_numbers=dims, preferred_element_type=F32)
    return dot(lh, rh) + (dot(lh, rl) + dot(ll, rh))


def dot_wide(left, right, dims=NN):
    return dot_parts(split(left), split(right), dims)


def inverse_block(block):
    width = block.shape[1]
    rows = lax.broadcasted_iota(jnp.int32, (8, width), 0)
    lanes = lax.broadcasted_iota(jnp.int32, (8, width), 1)

    def spread(value):
        return jnp.broadcast_to(value, (8, width))

    def key(i, j):
        return (i, j) if i <= j else (j, i)

    groups = [block[8 * i : 8 * i + 8] for i in range(width // 8)]
    for g, panel in enumerate(groups):
        panel = groups[g]
        first = 8 * g
        columns = [spread(panel[:, first + j : first + j + 1]) for j in range(8)]
        pivot = {(i, j): spread(columns[j][i : i + 1, :]) for j in range(8) for i in range(j + 1)}
        for k in range(8):
            inverse = 1.0 / pivot[k, k]
            old = {i: pivot[key(i, k)] for i in range(8) if i != k}
            scaled = {i: old[i] * inverse for i in old}
            for j in range(8):
                for i in range(j + 1):
                    if i != k and j != k:
                        pivot[i, j] = pivot[i, j] - scaled[i] * old[j]
            for i in old:
                pivot[key(i, k)] = scaled[i]
            pivot[k, k] = -inverse
        turned = []
        for j in range(8):
            column = pivot[key(7, j)]
            for i in range(6, -1, -1):
                column = jnp.where(rows == i, pivot[key(i, j)], column)
            turned.append(-column)
        solved = turned[0] * spread(panel[:1, :])
        for j in range(1, 8):
            solved = solved + turned[j] * spread(panel[j : j + 1, :])
        for j in range(8):
            solved = jnp.where(lanes == first + j, turned[j], solved)
        lines = [spread(solved[j : j + 1, :]) for j in range(8)]
        inside = (lanes >= first) & (lanes < first + 8)
        for i in [*range(g + 1, width // 8), *range(g)]:
            terms = [groups[i][:, first + j : first + j + 1] * lines[j] for j in range(8)]
            even = (terms[0] + terms[2]) + (terms[4] + terms[6])
            odd = (terms[1] + terms[3]) + (terms[5] + terms[7])
            groups[i] = jnp.where(inside, 0.0, groups[i]) - (even + odd)
        groups[g] = solved
    return jnp.concatenate(groups, axis=0)


def as_column(row):
    return jnp.broadcast_to(row, (8, row.shape[1])).T[:, :1]


def stack_columns(value):
    return jnp.concatenate(split(value), axis=1)


def stack_rows(value):
    high, low = split(value)
    return jnp.concatenate([high, high], axis=0), jnp.concatenate([low, low], axis=0)


def dot_stacked(left, right):
    high, low = right
    dot = functools.partial(jnp.dot, preferred_element_type=F32)
    return dot(left, high) + dot(left, low)


CHUNKS = [slice(i * 256, (i + 1) * 256) for i in range(WIDTH // 256)]
ALL = slice(None)


def on_device(embeds, counts):
    block_rows = embeds[0]
    rows = block_rows.shape[0]
    vmem = pl.BlockSpec(memory_space=pltpu.VMEM)
    dma = pltpu.SemaphoreType.DMA
    half, square = (HALF, WIDTH), (WIDTH, WIDTH)
    gradient, corr = pl.pallas_call(
        fused_kernel,
        out_shape=(jax.ShapeDtypeStruct(block_rows.shape, BF16), jax.ShapeDtypeStruct((8, 128), F32)),
        in_specs=[pl.BlockSpec(memory_space=pltpu.SMEM), vmem],
        out_specs=(vmem, vmem),
        scratch_shapes=[
            pltpu.VMEM((rows, WIDTH), BF16),
            pltpu.VMEM((WIDTH, rows), BF16),
            pltpu.VMEM((rows, WIDTH), BF16),
            pltpu.VMEM((rows, WIDTH), BF16),
            pltpu.VMEM(half, F32),
            pltpu.VMEM(half, F32),
            pltpu.VMEM(half, F32),
            pltpu.VMEM(square, F32),
            pltpu.VMEM((6, 3, 64, WIDTH), F32),
            pltpu.VMEM((6, 64, WIDTH), F32),
            pltpu.VMEM((6, 3, 16, WIDTH), F32),
            pltpu.VMEM((6, 16, WIDTH), F32),
            pltpu.VMEM((3, 7, 2, 16, 128), F32),
            pltpu.VMEM((6, 16, WIDTH), F32),
            pltpu.VMEM((SUB, 8, WIDTH), F32),
            pltpu.VMEM((YS, 8, WIDTH), F32),
            pltpu.VMEM((ZS, 8, WIDTH), F32),
            pltpu.VMEM(square, F32),
            pltpu.VMEM((2, *square), BF16),
            pltpu.VMEM((2, *square), BF16),
            pltpu.VMEM((rows, WIDTH), BF16),
            pltpu.VMEM((BLOCK, BLOCK), F32),
            pltpu.VMEM((WIDTH, 2 * BLOCK), BF16),
            pltpu.VMEM((2 * BLOCK, WIDTH), BF16),
            pltpu.VMEM((2 * BLOCK, WIDTH), BF16),
            pltpu.VMEM((2, 8, 128), F32),
            dma((6, 26)),
            dma((6, 26)),
            dma((13,)),
            dma((13,)),
            dma((4,)),
            dma((4,)),
        ],
        compiler_params=pltpu.CompilerParams(collective_id=0, has_side_effects=True, vmem_limit_bytes=60 * 2**20),
        name="fused",
    )(counts, block_rows)
    return gradient[None], corr[0, 0]


def solution(mesh):
    placed = (P("tower", ("depth", "sub"), None), P(("depth", "sub")))
    return jax.shard_map(
        on_device,
        mesh=mesh,
        in_specs=placed,
        out_specs=(P("tower", ("depth", "sub"), None), P()),
        check_vma=False,
    )
```

```python
import functools

import jax
import jax.numpy as jnp
from jax import lax
from jax.experimental import pallas as pl
from jax.experimental.pallas import tpu as pltpu
from jax.sharding import PartitionSpec as P

REG = 0.001
MESH = pl.DeviceIdType.MESH
F32, BF16 = jnp.float32, jnp.bfloat16
WIDTH = 1024
HALF = WIDTH // 2
TN = (((0,), (0,)), ((), ()))
NN = (((1,), (0,)), ((), ()))
NT = (((1,), (1,)), ((), ()))
SUB, YS, ZS = 4, 4, 8
BLOCK = 128


def fused_kernel(
    count_ref, x_ref, out_ref, corr_ref,
    own, own_t, raw, other, q_src, q_sum, c_src, c_sum,
    first_in, first_sum, second_in, second_sum, third_in, third_out, e_x, e_y, e_z,
    a_ref, a_parts, o_parts, residual, ready, side_parts, line_high, line_low, corr_box,
    sends, recvs, e_sends, e_recvs, pair_sends, pair_recvs,
):
    tower = lax.axis_index("tower")
    depth = lax.axis_index("depth")
    x = lax.axis_index("sub")
    y, z = depth // ZS, lax.rem(depth, ZS)
    rows = x_ref.shape[0]

    def at_x(p):
        return (tower, depth, p)

    def at_y(p):
        return (tower, p * ZS + z, x)

    def at_z(p):
        return (tower, y * ZS + p, x)

    partner = (1 - tower, depth, x)
    barrier = pltpu.get_barrier_semaphore()
    peers = [partner]
    peers += [at_x(lax.rem(x + d, SUB)) for d in range(1, SUB)]
    peers += [at_y(lax.rem(y + d, YS)) for d in range(1, YS)]
    peers += [at_z(lax.rem(z + d, ZS)) for d in range(1, ZS)]
    for peer in peers:
        pl.semaphore_signal(barrier, inc=1, device_id=peer, device_id_type=MESH)
    def remote(src, dst, send, recv, device):
        return pltpu.make_async_remote_copy(
            src_ref=src, dst_ref=dst, send_sem=send, recv_sem=recv, device_id=device, device_id_type=MESH
        )

    count = count_ref[0]

    def mask_into(src, dst):
        def body(i, carry):
            part = pl.ds(pl.multiple_of(i * 128, 128), 128)
            row = lax.broadcasted_iota(jnp.int32, (128, WIDTH), 0) + i * 128
            dst[part, :] = jnp.where(row < count, src[part, :].astype(F32), 0.0).astype(BF16)
            return carry

        lax.fori_loop(0, rows // 128, body, 0)

    def dot(a, b):
        return jnp.dot(a, b, preferred_element_type=F32)

    mask_into(x_ref, own)

    def turn(i, carry):
        part = pl.ds(pl.multiple_of(i * 128, 128), 128)
        own_t[part, :] = own[:, part].T
        return carry

    lax.fori_loop(0, WIDTH // 128, turn, 0)

    pl.semaphore_wait(barrier, len(peers))
    swap = remote(x_ref, raw, pair_sends.at[0], pair_recvs.at[0], partner)
    swap.start()

    r = lax.broadcasted_iota(jnp.int32, (HALF, HALF), 0)
    c = lax.broadcasted_iota(jnp.int32, (HALF, HALF), 1)

    cross_out = c_sum.at[pl.ds(pl.multiple_of(tower * HALF, HALF), HALF), :]
    streams = [(q_src, q_sum, h, slice(0, HALF)) for h in range(2)]
    streams += [(q_src, q_sum, h, slice(HALF, WIDTH)) for h in range(2)]
    streams += [(c_src, cross_out, h, slice(0, WIDTH)) for h in range(2)]

    def place(s):
        return ((x, at_x), (y, at_y)) if streams[s][2] == 0 else ((y, at_y), (x, at_x))

    def wide(s):
        return slice(0, HALF if s < 4 else WIDTH)

    def rows_of(first_row, size):
        return pl.ds(pl.multiple_of(first_row, size), size)

    def share(s, p):
        if s < 4:
            return rows_of(p // 4 * 8, 8), pl.ds(pl.multiple_of(lax.rem(p, 4) * 128, 128), 128)
        return slice(0, 16), pl.ds(pl.multiple_of(p * 128, 128), 128)

    def link(s, stage, src, dst, device):
        return remote(src, dst, sends.at[s, stage], recvs.at[s, stage], device)

    def first(s):
        src, _, half, columns = streams[s]
        (me, at), _ = place(s)
        copies = []
        for d in range(1, 4):
            to = lax.rem(me + d, 4)
            part = src.at[rows_of(half * 256 + to * 64, 64), columns]
            copies.append(link(s, d - 1, part, first_in.at[s, d - 1, :, wide(s)], at(to)))
        return copies

    def second(s):
        _, (me, at) = place(s)
        copies = []
        for d in range(1, 4):
            to = lax.rem(me + d, 4)
            part = first_sum.at[s, rows_of(to * 16, 16), wide(s)]
            copies.append(link(s, d + 2, part, second_in.at[s, d - 1, :, wide(s)], at(to)))
        return copies

    def third(s):
        copies = []
        for d in range(1, ZS):
            to = lax.rem(z + d, ZS)
            some_rows, columns = share(s, to)
            part = second_sum.at[s : s + 2, some_rows, columns]
            copies.append(link(s, d + 5, part, third_in.at[s // 2, d - 1, :, : 8 if s < 4 else 16, :], at_z(to)))
        return copies

    def spot(s):
        _, out, half, columns = streams[s]
        (p, _), (q, _) = place(s)
        return out, half * 256 + p * 64, half * 256 + p * 64 + q * 16, columns

    def gather_third(s):
        some_rows, columns = share(s, z)
        here = third_out.at[s : s + 2, some_rows, columns]
        return [link(s, d + 12, here, here, at_z(lax.rem(z + d, ZS))) for d in range(1, ZS)]

    def put_third(s):
        out, _, row, columns = spot(s)
        out[rows_of(row, 16), columns] = third_out[s, :, wide(s)]

    def gather_second(s):
        out, _, row, columns = spot(s)
        _, (me, at) = place(s)
        here = out.at[rows_of(row, 16), columns]
        return [link(s, d + 19, here, here, at(lax.rem(me + d, 4))) for d in range(1, 4)]

    def gather_first(s):
        out, row, _, columns = spot(s)
        (me, at), _ = place(s)
        here = out.at[rows_of(row, 64), columns]
        return [link(s, d + 22, here, here, at(lax.rem(me + d, 4))) for d in range(1, 4)]

    def start(copies):
        for copy in copies:
            copy.start()
        return copies

    def arrive(copies):
        for copy in copies:
            copy.wait()

    def sum_first(s):
        src, _, half, columns = streams[s]
        (me, _), _ = place(s)
        mine = src[rows_of(half * 256 + me * 64, 64), columns]
        came = [first_in[s, d, :, wide(s)] for d in range(3)]
        first_sum[s, :, wide(s)] = (mine + came[0]) + (came[1] + came[2])

    def sum_second(s):
        _, (me, _) = place(s)
        mine = first_sum[s, rows_of(me * 16, 16), wide(s)]
        came = [second_in[s, d, :, wide(s)] for d in range(3)]
        second_sum[s, :, wide(s)] = (mine + came[0]) + (came[1] + came[2])

    def sum_third(s):
        some_rows, columns = share(s, z)
        total = second_sum[s : s + 2, some_rows, columns]
        for d in range(ZS - 1):
            total = total + third_in[s // 2, d, :, : 8 if s < 4 else 16, :]
        third_out[s : s + 2, some_rows, columns] = total

    q_first = []
    diagonal = jnp.zeros((1, HALF), F32)
    for h in range(2):
        here, below = slice(h * 256, h * 256 + 256), slice(HALF + h * 256, HALF + h * 256 + 256)
        upper = dot(own_t[here, :], own[:, :HALF])
        lower = dot(own_t[below, :], own[:, HALF:])
        q_src[here, :HALF] = jnp.where(r[here] >= c[here], upper, lower)
        diagonal = diagonal + jnp.sum(jnp.where(r[here] == c[here], lower, 0.0), axis=0, keepdims=True)
        q_first.append(start(first(h)))
    for h in range(2):
        here, below = slice(h * 256, h * 256 + 256), slice(HALF + h * 256, HALF + h * 256 + 256)
        q_src[here, HALF:] = dot(own_t[below, :], own[:, :HALF])
        q_first.append(start(first(2 + h)))

    swap.wait()
    mask_into(raw, other)
    ones = jnp.ones((8, rows), BF16)
    own_sum = dot(ones, own[...])[:1]
    other_sum = dot(ones, other[...])[:1]
    is_log = tower == 0
    e_x[x] = jnp.concatenate(
        [
            jnp.where(is_log, own_sum, other_sum),
            jnp.where(is_log, other_sum, own_sum),
            jnp.concatenate([diagonal, diagonal], axis=1),
            jnp.full((5, WIDTH), count, jnp.int32).astype(F32),
        ],
        axis=0,
    )
    e_copies = start(
        [remote(e_x.at[x], e_x.at[x], e_sends.at[d - 1], e_recvs.at[d - 1], at_x(lax.rem(x + d, SUB))) for d in range(1, SUB)]
    )

    for s, copies in enumerate(q_first):
        arrive(copies)
        sum_first(s)
        start(second(s))
    arrive(e_copies)
    e_y[y] = (e_x[0] + e_x[1]) + (e_x[2] + e_x[3])
    e_copies = start(
        [remote(e_y.at[y], e_y.at[y], e_sends.at[d + 2], e_recvs.at[d + 2], at_y(lax.rem(y + d, YS))) for d in range(1, YS)]
    )
    @pl.when(is_log)
    def _():
        c_src[...] = dot(own_t[:HALF, :], other[...])

    @pl.when(tower == 1)
    def _():
        c_src[...] = lax.dot_general(other[:, HALF:], own[...], TN, preferred_element_type=F32)

    for s in (4, 5):
        start(first(s))
    for pair in (0, 2):
        for s in (pair, pair + 1):
            arrive(second(s))
            sum_second(s)
        start(third(pair))
    arrive(e_copies)
    e_z[z] = (e_y[0] + e_y[1]) + (e_y[2] + e_y[3])
    e_copies = start(
        [remote(e_z.at[z], e_z.at[z], e_sends.at[d + 5], e_recvs.at[d + 5], at_z(lax.rem(z + d, ZS))) for d in range(1, ZS)]
    )
    for pair in (0, 2):
        arrive(third(pair))
        sum_third(pair)
        start(gather_third(pair))
    for pair in (0, 2):
        arrive(gather_third(pair))
        for s in (pair, pair + 1):
            put_third(s)
            start(gather_second(s))
    for s in range(4):
        arrive(gather_second(s))
        start(gather_first(s))
    arrive(e_copies)
    sums = e_z[0]
    for d in range(1, ZS):
        sums = sums + e_z[d]
    for s in (0, 1):
        arrive(gather_first(s))

    count_total = sums[3:4, :1]
    own_total = jnp.where(is_log, sums[0:1], sums[1:2])
    own_mean = own_total / count_total
    other_mean = jnp.where(is_log, sums[1:2], sums[0:1]) / count_total
    column = as_column(own_total)
    eye = jnp.where(r == c, REG, 0.0)

    def covariance(gram, i, j):
        outer = column[i * HALF : (i + 1) * HALF] * own_mean[:, j * HALF : (j + 1) * HALF]
        value = (gram - outer) / (count_total - 1.0)
        a_ref[i * HALF : (i + 1) * HALF, j * HALF : (j + 1) * HALF] = value + eye if i == j else value

    shared = q_sum[:, :HALF]
    turned = shared.T
    covariance(jnp.where(r >= c, shared, turned), 0, 0)
    covariance(jnp.where(r == c, sums[2:3, :HALF], jnp.where(r > c, turned, shared)), 1, 1)
    ready[...] = inverse_block(a_ref[:BLOCK, :BLOCK])
    for s in (2, 3):
        arrive(gather_first(s))
    covariance(q_sum[:, HALF:], 1, 0)
    covariance(q_sum[:, HALF:].T, 0, 1)

    across = remote(cross_out, cross_out, pair_sends.at[1], pair_recvs.at[1], partner)

    def cross_moves(k):
        @pl.when(k == 0)
        def _():
            for s in (4, 5):
                arrive(first(s))
                sum_first(s)
                start(second(s))

        @pl.when(k == 1)
        def _():
            for s in (4, 5):
                arrive(second(s))
                sum_second(s)
            start(third(4))

        @pl.when(k == 2)
        def _():
            arrive(third(4))
            sum_third(4)
            start(gather_third(4))

        @pl.when(k == 3)
        def _():
            arrive(gather_third(4))
            for s in (4, 5):
                put_third(s)
                start(gather_second(s))

        @pl.when(k == 4)
        def _():
            for s in (4, 5):
                arrive(gather_second(s))
                start(gather_first(s))

        @pl.when(k == 6)
        def _():
            for s in (4, 5):
                arrive(gather_first(s))
            across.start()

    def step(k, carry):
        cross_moves(k)
        here = pl.ds(pl.multiple_of(k * BLOCK, BLOCK), BLOCK)
        after = lax.rem(k + 1, WIDTH // BLOCK) * BLOCK
        after = pl.ds(pl.multiple_of(after, BLOCK), BLOCK)
        inverse = ready[...]
        left = stack_columns(inverse)
        follow = a_ref[after, after] - dot_stacked(
            stack_columns(a_ref[after, here]), stack_rows(dot_stacked(left, stack_rows(a_ref[here, after])))
        )
        side = a_ref[:, here]
        solved = dot_stacked(left, stack_rows(a_ref[here, :]))
        a_ref[:, here] = jnp.zeros((WIDTH, BLOCK), F32)
        a_ref[here, :] = solved
        a_ref[here, here] = inverse
        line_high[...], line_low[...] = stack_rows(a_ref[here, :])
        row = lax.broadcasted_iota(jnp.int32, (WIDTH, BLOCK), 0) - k * BLOCK
        side_parts[...] = stack_columns(jnp.where((row >= 0) & (row < BLOCK), 0.0, side))
        for i in range(4):
            for j in range(4):
                rows_part, columns_part = slice(i * 256, (i + 1) * 256), slice(j * 256, (j + 1) * 256)
                a_ref[rows_part, columns_part] = a_ref[rows_part, columns_part] - dot_stacked(
                    side_parts[rows_part, :], (line_high[:, columns_part], line_low[:, columns_part])
                )
        ready[...] = inverse_block(follow)
        return carry

    lax.fori_loop(0, WIDTH // BLOCK, step, 0)

    for part in CHUNKS:
        high, low = split(a_ref[part, :])
        a_parts[0, part, :] = high
        a_parts[1, part, :] = low
    trade = remote(a_parts, o_parts, pair_sends.at[3], pair_recvs.at[3], partner)
    trade.start()
    across.wait()
    p_high, p_low = own_t, raw
    log_column = as_column(sums[0:1])
    image_mean = sums[1:2] / count_total

    def cross_covariance(some_rows, some_columns):
        outer = log_column[some_rows] * image_mean[:, some_columns]
        return (c_sum[some_rows, some_columns] - outer) / (count_total - 1.0)

    for part in CHUNKS:

        @pl.when(is_log)
        def _():
            cross = split(cross_covariance(ALL, part))
            p_high[:, part], p_low[:, part] = split(dot_parts((a_parts[0], a_parts[1]), cross, NN))

        @pl.when(tower == 1)
        def _():
            cross = split(cross_covariance(part, ALL))
            p_high[:, part], p_low[:, part] = split(dot_parts((a_parts[0], a_parts[1]), cross, NT))

    mean_parts = split(jnp.broadcast_to(own_mean, (8, WIDTH)))
    for part in CHUNKS:
        high, low = p_high[:, part], p_low[:, part]
        shift = dot_parts(mean_parts, (high, low), NN)[:1]
        left = (other[:, part].astype(F32) - (dot(own[...], high) + dot(own[...], low))) - (other_mean[:, part] - shift)
        residual[:, part] = left.astype(BF16)

    trade.wait()
    m_high, m_low = a_parts.at[0], a_parts.at[1]
    corr = jnp.zeros((1, 256), F32)
    for part in CHUNKS:
        back = dot_parts((o_parts[0], o_parts[1]), (p_high[part, :], p_low[part, :]), NT)
        m_high[:, part], m_low[:, part] = split(back)
        corr = corr + jnp.sum(back * cross_covariance(ALL, part), axis=0, keepdims=True)
    corr_box[tower] = jnp.broadcast_to(jnp.sum(corr, axis=1, keepdims=True) / WIDTH, (8, 128))
    tell = remote(corr_box.at[tower], corr_box.at[tower], pair_sends.at[2], pair_recvs.at[2], partner)
    tell.start()
    for part in CHUNKS:
        value = dot(residual[...], m_high[:, part]) + dot(residual[...], m_low[:, part])
        out_ref[:, part] = value.astype(BF16)
    tell.wait()
    corr_ref[...] = corr_box[1, :1, :1]


def split(value):
    high = value.astype(BF16)
    return high, (value - high.astype(F32)).astype(BF16)


def dot_parts(left, right, dims):
    (lh, ll), (rh, rl) = left, right
    dot = functools.partial(lax.dot_general, dimension_numbers=dims, preferred_element_type=F32)
    return dot(lh, rh) + (dot(lh, rl) + dot(ll, rh))


def dot_wide(left, right, dims=NN):
    return dot_parts(split(left), split(right), dims)


def inverse_block(block):
    width = block.shape[1]
    rows = lax.broadcasted_iota(jnp.int32, (8, width), 0)
    lanes = lax.broadcasted_iota(jnp.int32, (8, width), 1)

    def spread(value):
        return jnp.broadcast_to(value, (8, width))

    def key(i, j):
        return (i, j) if i <= j else (j, i)

    groups = [block[8 * i : 8 * i + 8] for i in range(width // 8)]
    for g, panel in enumerate(groups):
        panel = groups[g]
        first = 8 * g
        columns = [spread(panel[:, first + j : first + j + 1]) for j in range(8)]
        pivot = {(i, j): spread(columns[j][i : i + 1, :]) for j in range(8) for i in range(j + 1)}
        for k in range(0, 8, 2):
            one, both, two = pivot[k, k], pivot[k, k + 1], pivot[k + 1, k + 1]
            scale = 1.0 / (one * two - both * both)
            one, both, two = two * scale, -(both * scale), one * scale
            rest = [i for i in range(8) if i not in (k, k + 1)]
            old = {i: (pivot[key(i, k)], pivot[key(i, k + 1)]) for i in rest}
            scaled = {i: (one * old[i][0] + both * old[i][1], both * old[i][0] + two * old[i][1]) for i in rest}
            for j in rest:
                for i in rest:
                    if i <= j:
                        pivot[i, j] = pivot[i, j] - (scaled[i][0] * old[j][0] + scaled[i][1] * old[j][1])
            for i in rest:
                pivot[key(i, k)], pivot[key(i, k + 1)] = scaled[i]
            pivot[k, k], pivot[k, k + 1], pivot[k + 1, k + 1] = -one, -both, -two
        turned = []
        for j in range(8):
            column = pivot[key(7, j)]
            for i in range(6, -1, -1):
                column = jnp.where(rows == i, pivot[key(i, j)], column)
            turned.append(-column)
        solved = turned[0] * spread(panel[:1, :])
        for j in range(1, 8):
            solved = solved + turned[j] * spread(panel[j : j + 1, :])
        for j in range(8):
            solved = jnp.where(lanes == first + j, turned[j], solved)
        lines = [spread(solved[j : j + 1, :]) for j in range(8)]
        inside = (lanes >= first) & (lanes < first + 8)
        for i in [*range(g + 1, width // 8), *range(g)]:
            terms = [groups[i][:, first + j : first + j + 1] * lines[j] for j in range(8)]
            even = (terms[0] + terms[2]) + (terms[4] + terms[6])
            odd = (terms[1] + terms[3]) + (terms[5] + terms[7])
            groups[i] = jnp.where(inside, 0.0, groups[i]) - (even + odd)
        groups[g] = solved
    return jnp.concatenate(groups, axis=0)


def as_column(row):
    return jnp.broadcast_to(row, (8, row.shape[1])).T[:, :1]


def stack_columns(value):
    return jnp.concatenate(split(value), axis=1)


def stack_rows(value):
    high, low = split(value)
    return jnp.concatenate([high, high], axis=0), jnp.concatenate([low, low], axis=0)


def dot_stacked(left, right):
    high, low = right
    dot = functools.partial(jnp.dot, preferred_element_type=F32)
    return dot(left, high) + dot(left, low)


CHUNKS = [slice(i * 256, (i + 1) * 256) for i in range(WIDTH // 256)]
ALL = slice(None)


def on_device(embeds, counts):
    block_rows = embeds[0]
    rows = block_rows.shape[0]
    vmem = pl.BlockSpec(memory_space=pltpu.VMEM)
    dma = pltpu.SemaphoreType.DMA
    half, square = (HALF, WIDTH), (WIDTH, WIDTH)
    gradient, corr = pl.pallas_call(
        fused_kernel,
        out_shape=(jax.ShapeDtypeStruct(block_rows.shape, BF16), jax.ShapeDtypeStruct((1, 1), F32)),
        in_specs=[pl.BlockSpec(memory_space=pltpu.SMEM), vmem],
        out_specs=(vmem, vmem),
        scratch_shapes=[
            pltpu.VMEM((rows, WIDTH), BF16),
            pltpu.VMEM((WIDTH, rows), BF16),
            pltpu.VMEM((rows, WIDTH), BF16),
            pltpu.VMEM((rows, WIDTH), BF16),
            pltpu.VMEM(half, F32),
            pltpu.VMEM(half, F32),
            pltpu.VMEM(half, F32),
            pltpu.VMEM(square, F32),
            pltpu.VMEM((6, 3, 64, WIDTH), F32),
            pltpu.VMEM((6, 64, WIDTH), F32),
            pltpu.VMEM((6, 3, 16, WIDTH), F32),
            pltpu.VMEM((6, 16, WIDTH), F32),
            pltpu.VMEM((3, 7, 2, 16, 128), F32),
            pltpu.VMEM((6, 16, WIDTH), F32),
            pltpu.VMEM((SUB, 8, WIDTH), F32),
            pltpu.VMEM((YS, 8, WIDTH), F32),
            pltpu.VMEM((ZS, 8, WIDTH), F32),
            pltpu.VMEM(square, F32),
            pltpu.VMEM((2, *square), BF16),
            pltpu.VMEM((2, *square), BF16),
            pltpu.VMEM((rows, WIDTH), BF16),
            pltpu.VMEM((BLOCK, BLOCK), F32),
            pltpu.VMEM((WIDTH, 2 * BLOCK), BF16),
            pltpu.VMEM((2 * BLOCK, WIDTH), BF16),
            pltpu.VMEM((2 * BLOCK, WIDTH), BF16),
            pltpu.VMEM((2, 8, 128), F32),
            dma((6, 26)),
            dma((6, 26)),
            dma((13,)),
            dma((13,)),
            dma((4,)),
            dma((4,)),
        ],
        compiler_params=pltpu.CompilerParams(collective_id=0, has_side_effects=True, vmem_limit_bytes=60 * 2**20),
        name="fused",
    )(counts, block_rows)
    valid = lax.iota(jnp.int32, rows) < counts[0]
    gradient = jnp.where(valid[:, None], gradient, jnp.zeros_like(gradient))
    return gradient[None], corr.reshape(())


def solution(mesh):
    placed = (P("tower", ("depth", "sub"), None), P(("depth", "sub")))
    return jax.shard_map(
        on_device,
        mesh=mesh,
        in_specs=placed,
        out_specs=(P("tower", ("depth", "sub"), None), P()),
        check_vma=False,
    )
```

```python
import functools

import jax
import jax.numpy as jnp
from jax import lax
from jax.experimental import pallas as pl
from jax.experimental.pallas import tpu as pltpu
from jax.sharding import PartitionSpec as P

REG = 0.001
MESH = pl.DeviceIdType.MESH
F32, BF16 = jnp.float32, jnp.bfloat16
WIDTH = 1024
HALF = WIDTH // 2
TN = (((0,), (0,)), ((), ()))
NN = (((1,), (0,)), ((), ()))
NT = (((1,), (1,)), ((), ()))
SUB, YS, ZS = 4, 4, 8
BLOCK = 128


def fused_kernel(
    count_ref, x_ref, out_ref, corr_ref,
    own, own_t, raw, other, q_src, q_sum, c_src, c_sum,
    first_in, first_sum, second_in, second_sum, third_in, third_out, e_x, e_y, e_z,
    a_ref, a_parts, o_parts, residual, ready, side_parts, line_high, line_low, corr_box,
    sends, recvs, e_sends, e_recvs, pair_sends, pair_recvs,
):
    tower = lax.axis_index("tower")
    depth = lax.axis_index("depth")
    x = lax.axis_index("sub")
    y, z = depth // ZS, lax.rem(depth, ZS)
    rows = x_ref.shape[0]

    def at_x(p):
        return (tower, depth, p)

    def at_y(p):
        return (tower, p * ZS + z, x)

    def at_z(p):
        return (tower, y * ZS + p, x)

    partner = (1 - tower, depth, x)
    barrier = pltpu.get_barrier_semaphore()
    peers = [partner]
    peers += [at_x(lax.rem(x + d, SUB)) for d in range(1, SUB)]
    peers += [at_y(lax.rem(y + d, YS)) for d in range(1, YS)]
    peers += [at_z(lax.rem(z + d, ZS)) for d in range(1, ZS)]
    for peer in peers:
        pl.semaphore_signal(barrier, inc=1, device_id=peer, device_id_type=MESH)
    def remote(src, dst, send, recv, device):
        return pltpu.make_async_remote_copy(
            src_ref=src, dst_ref=dst, send_sem=send, recv_sem=recv, device_id=device, device_id_type=MESH
        )

    count = count_ref[0]

    def mask_into(src, dst):
        def body(i, carry):
            part = pl.ds(pl.multiple_of(i * 128, 128), 128)
            row = lax.broadcasted_iota(jnp.int32, (128, WIDTH), 0) + i * 128
            dst[part, :] = jnp.where(row < count, src[part, :].astype(F32), 0.0).astype(BF16)
            return carry

        lax.fori_loop(0, rows // 128, body, 0)

    def dot(a, b):
        return jnp.dot(a, b, preferred_element_type=F32)

    mask_into(x_ref, own)

    def turn(i, carry):
        part = pl.ds(pl.multiple_of(i * 128, 128), 128)
        own_t[part, :] = own[:, part].T
        return carry

    lax.fori_loop(0, WIDTH // 128, turn, 0)

    pl.semaphore_wait(barrier, len(peers))
    swap = remote(x_ref, raw, pair_sends.at[0], pair_recvs.at[0], partner)
    swap.start()

    r = lax.broadcasted_iota(jnp.int32, (HALF, HALF), 0)
    c = lax.broadcasted_iota(jnp.int32, (HALF, HALF), 1)

    cross_out = c_sum.at[pl.ds(pl.multiple_of(tower * HALF, HALF), HALF), :]
    streams = [(q_src, q_sum, h, slice(0, HALF)) for h in range(2)]
    streams += [(q_src, q_sum, h, slice(HALF, WIDTH)) for h in range(2)]
    streams += [(c_src, cross_out, h, slice(0, WIDTH)) for h in range(2)]

    def place(s):
        return ((x, at_x), (y, at_y)) if streams[s][2] == 0 else ((y, at_y), (x, at_x))

    def wide(s):
        return slice(0, HALF if s < 4 else WIDTH)

    def rows_of(first_row, size):
        return pl.ds(pl.multiple_of(first_row, size), size)

    def share(s, p):
        if s < 4:
            return rows_of(p // 4 * 8, 8), pl.ds(pl.multiple_of(lax.rem(p, 4) * 128, 128), 128)
        return slice(0, 16), pl.ds(pl.multiple_of(p * 128, 128), 128)

    def link(s, stage, src, dst, device):
        return remote(src, dst, sends.at[s, stage], recvs.at[s, stage], device)

    def first(s):
        src, _, half, columns = streams[s]
        (me, at), _ = place(s)
        copies = []
        for d in range(1, 4):
            to = lax.rem(me + d, 4)
            part = src.at[rows_of(half * 256 + to * 64, 64), columns]
            copies.append(link(s, d - 1, part, first_in.at[s, d - 1, :, wide(s)], at(to)))
        return copies

    def second(s):
        _, (me, at) = place(s)
        copies = []
        for d in range(1, 4):
            to = lax.rem(me + d, 4)
            part = first_sum.at[s, rows_of(to * 16, 16), wide(s)]
            copies.append(link(s, d + 2, part, second_in.at[s, d - 1, :, wide(s)], at(to)))
        return copies

    def third(s):
        copies = []
        for d in range(1, ZS):
            to = lax.rem(z + d, ZS)
            some_rows, columns = share(s, to)
            part = second_sum.at[s : s + 2, some_rows, columns]
            copies.append(link(s, d + 5, part, third_in.at[s // 2, d - 1, :, : 8 if s < 4 else 16, :], at_z(to)))
        return copies

    def spot(s):
        _, out, half, columns = streams[s]
        (p, _), (q, _) = place(s)
        return out, half * 256 + p * 64, half * 256 + p * 64 + q * 16, columns

    def gather_third(s):
        some_rows, columns = share(s, z)
        here = third_out.at[s : s + 2, some_rows, columns]
        return [link(s, d + 12, here, here, at_z(lax.rem(z + d, ZS))) for d in range(1, ZS)]

    def put_third(s):
        out, _, row, columns = spot(s)
        out[rows_of(row, 16), columns] = third_out[s, :, wide(s)]

    def gather_second(s):
        out, _, row, columns = spot(s)
        _, (me, at) = place(s)
        here = out.at[rows_of(row, 16), columns]
        return [link(s, d + 19, here, here, at(lax.rem(me + d, 4))) for d in range(1, 4)]

    def gather_first(s):
        out, row, _, columns = spot(s)
        (me, at), _ = place(s)
        here = out.at[rows_of(row, 64), columns]
        return [link(s, d + 22, here, here, at(lax.rem(me + d, 4))) for d in range(1, 4)]

    def start(copies):
        for copy in copies:
            copy.start()
        return copies

    def arrive(copies):
        for copy in copies:
            copy.wait()

    def sum_first(s):
        src, _, half, columns = streams[s]
        (me, _), _ = place(s)
        mine = src[rows_of(half * 256 + me * 64, 64), columns]
        came = [first_in[s, d, :, wide(s)] for d in range(3)]
        first_sum[s, :, wide(s)] = (mine + came[0]) + (came[1] + came[2])

    def sum_second(s):
        _, (me, _) = place(s)
        mine = first_sum[s, rows_of(me * 16, 16), wide(s)]
        came = [second_in[s, d, :, wide(s)] for d in range(3)]
        second_sum[s, :, wide(s)] = (mine + came[0]) + (came[1] + came[2])

    def sum_third(s):
        some_rows, columns = share(s, z)
        total = second_sum[s : s + 2, some_rows, columns]
        for d in range(ZS - 1):
            total = total + third_in[s // 2, d, :, : 8 if s < 4 else 16, :]
        third_out[s : s + 2, some_rows, columns] = total

    q_first = []
    diagonal = jnp.zeros((1, HALF), F32)
    for h in range(2):
        here, below = slice(h * 256, h * 256 + 256), slice(HALF + h * 256, HALF + h * 256 + 256)
        upper = dot(own_t[here, :], own[:, :HALF])
        lower = dot(own_t[below, :], own[:, HALF:])
        q_src[here, :HALF] = jnp.where(r[here] >= c[here], upper, lower)
        diagonal = diagonal + jnp.sum(jnp.where(r[here] == c[here], lower, 0.0), axis=0, keepdims=True)
        q_first.append(start(first(h)))
    for h in range(2):
        here, below = slice(h * 256, h * 256 + 256), slice(HALF + h * 256, HALF + h * 256 + 256)
        q_src[here, HALF:] = dot(own_t[below, :], own[:, :HALF])
        q_first.append(start(first(2 + h)))

    for s, copies in enumerate(q_first):
        arrive(copies)
        sum_first(s)
        start(second(s))

    swap.wait()
    mask_into(raw, other)
    ones = jnp.ones((8, rows), BF16)
    own_sum = dot(ones, own[...])[:1]
    other_sum = dot(ones, other[...])[:1]
    is_log = tower == 0
    e_x[x] = jnp.concatenate(
        [
            jnp.where(is_log, own_sum, other_sum),
            jnp.where(is_log, other_sum, own_sum),
            jnp.concatenate([diagonal, diagonal], axis=1),
            jnp.full((5, WIDTH), count, jnp.int32).astype(F32),
        ],
        axis=0,
    )
    e_copies = start(
        [remote(e_x.at[x], e_x.at[x], e_sends.at[d - 1], e_recvs.at[d - 1], at_x(lax.rem(x + d, SUB))) for d in range(1, SUB)]
    )

    @pl.when(is_log)
    def _():
        c_src[...] = dot(own_t[:HALF, :], other[...])

    @pl.when(tower == 1)
    def _():
        c_src[...] = lax.dot_general(other[:, HALF:], own[...], TN, preferred_element_type=F32)

    for s in (4, 5):
        start(first(s))
    for pair in (0, 2):
        for s in (pair, pair + 1):
            arrive(second(s))
            sum_second(s)
        start(third(pair))
    arrive(e_copies)
    e_y[y] = (e_x[0] + e_x[1]) + (e_x[2] + e_x[3])
    e_copies = start(
        [remote(e_y.at[y], e_y.at[y], e_sends.at[d + 2], e_recvs.at[d + 2], at_y(lax.rem(y + d, YS))) for d in range(1, YS)]
    )
    for pair in (0, 2):
        arrive(third(pair))
        sum_third(pair)
        start(gather_third(pair))
    arrive(e_copies)
    e_z[z] = (e_y[0] + e_y[1]) + (e_y[2] + e_y[3])
    e_copies = start(
        [remote(e_z.at[z], e_z.at[z], e_sends.at[d + 5], e_recvs.at[d + 5], at_z(lax.rem(z + d, ZS))) for d in range(1, ZS)]
    )
    for pair in (0, 2):
        arrive(gather_third(pair))
        for s in (pair, pair + 1):
            put_third(s)
            start(gather_second(s))
    for s in range(4):
        arrive(gather_second(s))
        start(gather_first(s))
    arrive(e_copies)
    sums = e_z[0]
    for d in range(1, ZS):
        sums = sums + e_z[d]
    for s in (0, 1):
        arrive(gather_first(s))

    count_total = sums[3:4, :1]
    per_sample = 1.0 / (count_total - 1.0)
    own_total = jnp.where(is_log, sums[0:1], sums[1:2])
    own_mean = own_total / count_total
    other_mean = jnp.where(is_log, sums[1:2], sums[0:1]) / count_total
    column = as_column(own_total)
    eye = jnp.where(r == c, REG, 0.0)

    def covariance(gram, i, j):
        outer = column[i * HALF : (i + 1) * HALF] * own_mean[:, j * HALF : (j + 1) * HALF]
        value = (gram - outer) * per_sample
        a_ref[i * HALF : (i + 1) * HALF, j * HALF : (j + 1) * HALF] = value + eye if i == j else value

    shared = q_sum[:, :HALF]
    turned = shared.T
    covariance(jnp.where(r >= c, shared, turned), 0, 0)
    covariance(jnp.where(r == c, sums[2:3, :HALF], jnp.where(r > c, turned, shared)), 1, 1)
    ready[...] = inverse_block(a_ref[:BLOCK, :BLOCK])
    for s in (2, 3):
        arrive(gather_first(s))
    covariance(q_sum[:, HALF:], 1, 0)
    covariance(q_sum[:, HALF:].T, 0, 1)

    across = remote(cross_out, cross_out, pair_sends.at[1], pair_recvs.at[1], partner)

    def cross_moves(k):
        @pl.when(k == 0)
        def _():
            for s in (4, 5):
                arrive(first(s))
                sum_first(s)
                start(second(s))

        @pl.when(k == 1)
        def _():
            for s in (4, 5):
                arrive(second(s))
                sum_second(s)
            start(third(4))

        @pl.when(k == 2)
        def _():
            arrive(third(4))
            sum_third(4)
            start(gather_third(4))

        @pl.when(k == 3)
        def _():
            arrive(gather_third(4))
            for s in (4, 5):
                put_third(s)
                start(gather_second(s))

        @pl.when(k == 4)
        def _():
            for s in (4, 5):
                arrive(gather_second(s))
                start(gather_first(s))

        @pl.when(k == 6)
        def _():
            for s in (4, 5):
                arrive(gather_first(s))
            across.start()

    def step(k, carry):
        cross_moves(k)
        here = pl.ds(pl.multiple_of(k * BLOCK, BLOCK), BLOCK)
        after = lax.rem(k + 1, WIDTH // BLOCK) * BLOCK
        after = pl.ds(pl.multiple_of(after, BLOCK), BLOCK)
        inverse = ready[...]
        left = stack_columns(inverse)
        follow = a_ref[after, after] - dot_stacked(
            stack_columns(a_ref[after, here]), stack_rows(dot_stacked(left, stack_rows(a_ref[here, after])))
        )
        side = a_ref[:, here]
        solved = dot_stacked(left, stack_rows(a_ref[here, :]))
        a_ref[:, here] = jnp.zeros((WIDTH, BLOCK), F32)
        a_ref[here, :] = solved
        a_ref[here, here] = inverse
        line_high[...], line_low[...] = stack_rows(a_ref[here, :])
        row = lax.broadcasted_iota(jnp.int32, (WIDTH, BLOCK), 0) - k * BLOCK
        side_parts[...] = stack_columns(jnp.where((row >= 0) & (row < BLOCK), 0.0, side))
        for i in range(4):
            for j in range(4):
                rows_part, columns_part = slice(i * 256, (i + 1) * 256), slice(j * 256, (j + 1) * 256)
                a_ref[rows_part, columns_part] = a_ref[rows_part, columns_part] - dot_stacked(
                    side_parts[rows_part, :], (line_high[:, columns_part], line_low[:, columns_part])
                )
        ready[...] = inverse_block(follow)
        return carry

    lax.fori_loop(0, WIDTH // BLOCK, step, 0)

    for part in CHUNKS:
        high, low = split(a_ref[part, :])
        a_parts[0, part, :] = high
        a_parts[1, part, :] = low
    trade = remote(a_parts, o_parts, pair_sends.at[3], pair_recvs.at[3], partner)
    trade.start()
    across.wait()
    p_high, p_low = own_t, raw
    log_column = as_column(sums[0:1])
    image_mean = sums[1:2] / count_total

    def cross_covariance(some_rows, some_columns):
        outer = log_column[some_rows] * image_mean[:, some_columns]
        return (c_sum[some_rows, some_columns] - outer) * per_sample

    for part in CHUNKS:

        @pl.when(is_log)
        def _():
            cross = split(cross_covariance(ALL, part))
            p_high[:, part], p_low[:, part] = split(dot_parts((a_parts[0], a_parts[1]), cross, NN))

        @pl.when(tower == 1)
        def _():
            cross = split(cross_covariance(part, ALL))
            p_high[:, part], p_low[:, part] = split(dot_parts((a_parts[0], a_parts[1]), cross, NT))

    mean_parts = split(jnp.broadcast_to(own_mean, (8, WIDTH)))
    for part in CHUNKS:
        high, low = p_high[:, part], p_low[:, part]
        shift = dot_parts(mean_parts, (high, low), NN)[:1]
        left = (other[:, part].astype(F32) - (dot(own[...], high) + dot(own[...], low))) - (other_mean[:, part] - shift)
        residual[:, part] = left.astype(BF16)

    trade.wait()
    m_high, m_low = a_parts.at[0], a_parts.at[1]
    corr = jnp.zeros((1, 256), F32)
    for part in CHUNKS:
        back = dot_parts((o_parts[0], o_parts[1]), (p_high[part, :], p_low[part, :]), NT)
        m_high[:, part], m_low[:, part] = split(back)
        corr = corr + jnp.sum(back * cross_covariance(ALL, part), axis=0, keepdims=True)
    corr_box[tower] = jnp.broadcast_to(jnp.sum(corr, axis=1, keepdims=True) / WIDTH, (8, 128))
    tell = remote(corr_box.at[tower], corr_box.at[tower], pair_sends.at[2], pair_recvs.at[2], partner)
    tell.start()
    for part in CHUNKS:
        value = dot(residual[...], m_high[:, part]) + dot(residual[...], m_low[:, part])
        out_ref[:, part] = value.astype(BF16)
    tell.wait()
    corr_ref[...] = corr_box[1, :1, :1]


def split(value):
    high = value.astype(BF16)
    return high, (value - high.astype(F32)).astype(BF16)


def dot_parts(left, right, dims):
    (lh, ll), (rh, rl) = left, right
    dot = functools.partial(lax.dot_general, dimension_numbers=dims, preferred_element_type=F32)
    return dot(lh, rh) + (dot(lh, rl) + dot(ll, rh))


def dot_wide(left, right, dims=NN):
    return dot_parts(split(left), split(right), dims)


def inverse_block(block):
    width = block.shape[1]
    rows = lax.broadcasted_iota(jnp.int32, (8, width), 0)
    lanes = lax.broadcasted_iota(jnp.int32, (8, width), 1)

    def spread(value):
        return jnp.broadcast_to(value, (8, width))

    def key(i, j):
        return (i, j) if i <= j else (j, i)

    groups = [block[8 * i : 8 * i + 8] for i in range(width // 8)]
    for g, panel in enumerate(groups):
        panel = groups[g]
        first = 8 * g
        columns = [spread(panel[:, first + j : first + j + 1]) for j in range(8)]
        pivot = {(i, j): spread(columns[j][i : i + 1, :]) for j in range(8) for i in range(j + 1)}
        for k in range(0, 8, 2):
            one, both, two = pivot[k, k], pivot[k, k + 1], pivot[k + 1, k + 1]
            scale = 1.0 / (one * two - both * both)
            one, both, two = two * scale, -(both * scale), one * scale
            rest = [i for i in range(8) if i not in (k, k + 1)]
            old = {i: (pivot[key(i, k)], pivot[key(i, k + 1)]) for i in rest}
            scaled = {i: (one * old[i][0] + both * old[i][1], both * old[i][0] + two * old[i][1]) for i in rest}
            for j in rest:
                for i in rest:
                    if i <= j:
                        pivot[i, j] = pivot[i, j] - (scaled[i][0] * old[j][0] + scaled[i][1] * old[j][1])
            for i in rest:
                pivot[key(i, k)], pivot[key(i, k + 1)] = scaled[i]
            pivot[k, k], pivot[k, k + 1], pivot[k + 1, k + 1] = -one, -both, -two
        turned = []
        for j in range(8):
            column = pivot[key(7, j)]
            for i in range(6, -1, -1):
                column = jnp.where(rows == i, pivot[key(i, j)], column)
            turned.append(-column)
        solved = turned[0] * spread(panel[:1, :])
        for j in range(1, 8):
            solved = solved + turned[j] * spread(panel[j : j + 1, :])
        for j in range(8):
            solved = jnp.where(lanes == first + j, turned[j], solved)
        lines = [spread(solved[j : j + 1, :]) for j in range(8)]
        inside = (lanes >= first) & (lanes < first + 8)
        for i in [*range(g + 1, width // 8), *range(g)]:
            terms = [groups[i][:, first + j : first + j + 1] * lines[j] for j in range(8)]
            even = (terms[0] + terms[2]) + (terms[4] + terms[6])
            odd = (terms[1] + terms[3]) + (terms[5] + terms[7])
            groups[i] = jnp.where(inside, 0.0, groups[i]) - (even + odd)
        groups[g] = solved
    return jnp.concatenate(groups, axis=0)


def as_column(row):
    return jnp.broadcast_to(row, (8, row.shape[1])).T[:, :1]


def stack_columns(value):
    return jnp.concatenate(split(value), axis=1)


def stack_rows(value):
    high, low = split(value)
    return jnp.concatenate([high, high], axis=0), jnp.concatenate([low, low], axis=0)


def dot_stacked(left, right):
    high, low = right
    dot = functools.partial(jnp.dot, preferred_element_type=F32)
    return dot(left, high) + dot(left, low)


CHUNKS = [slice(i * 256, (i + 1) * 256) for i in range(WIDTH // 256)]
ALL = slice(None)


def on_device(embeds, counts):
    block_rows = embeds[0]
    rows = block_rows.shape[0]
    vmem = pl.BlockSpec(memory_space=pltpu.VMEM)
    dma = pltpu.SemaphoreType.DMA
    half, square = (HALF, WIDTH), (WIDTH, WIDTH)
    gradient, corr = pl.pallas_call(
        fused_kernel,
        out_shape=(jax.ShapeDtypeStruct(block_rows.shape, BF16), jax.ShapeDtypeStruct((1, 1), F32)),
        in_specs=[pl.BlockSpec(memory_space=pltpu.SMEM), vmem],
        out_specs=(vmem, vmem),
        scratch_shapes=[
            pltpu.VMEM((rows, WIDTH), BF16),
            pltpu.VMEM((WIDTH, rows), BF16),
            pltpu.VMEM((rows, WIDTH), BF16),
            pltpu.VMEM((rows, WIDTH), BF16),
            pltpu.VMEM(half, F32),
            pltpu.VMEM(half, F32),
            pltpu.VMEM(half, F32),
            pltpu.VMEM(square, F32),
            pltpu.VMEM((6, 3, 64, WIDTH), F32),
            pltpu.VMEM((6, 64, WIDTH), F32),
            pltpu.VMEM((6, 3, 16, WIDTH), F32),
            pltpu.VMEM((6, 16, WIDTH), F32),
            pltpu.VMEM((3, 7, 2, 16, 128), F32),
            pltpu.VMEM((6, 16, WIDTH), F32),
            pltpu.VMEM((SUB, 8, WIDTH), F32),
            pltpu.VMEM((YS, 8, WIDTH), F32),
            pltpu.VMEM((ZS, 8, WIDTH), F32),
            pltpu.VMEM(square, F32),
            pltpu.VMEM((2, *square), BF16),
            pltpu.VMEM((2, *square), BF16),
            pltpu.VMEM((rows, WIDTH), BF16),
            pltpu.VMEM((BLOCK, BLOCK), F32),
            pltpu.VMEM((WIDTH, 2 * BLOCK), BF16),
            pltpu.VMEM((2 * BLOCK, WIDTH), BF16),
            pltpu.VMEM((2 * BLOCK, WIDTH), BF16),
            pltpu.VMEM((2, 8, 128), F32),
            dma((6, 26)),
            dma((6, 26)),
            dma((13,)),
            dma((13,)),
            dma((4,)),
            dma((4,)),
        ],
        compiler_params=pltpu.CompilerParams(collective_id=0, has_side_effects=True, vmem_limit_bytes=60 * 2**20),
        name="fused",
    )(counts, block_rows)
    valid = lax.iota(jnp.int32, rows) < counts[0]
    gradient = jnp.where(valid[:, None], gradient, jnp.zeros_like(gradient))
    return gradient[None], corr.reshape(())


def solution(mesh):
    placed = (P("tower", ("depth", "sub"), None), P(("depth", "sub")))
    return jax.shard_map(
        on_device,
        mesh=mesh,
        in_specs=placed,
        out_specs=(P("tower", ("depth", "sub"), None), P()),
        check_vma=False,
    )
```
